32 devices in a mesh: grp: 4 (over x, core), peak: 8 (over z, y).
Axes of the slice: x: 2, y: 2, z: 4, core: 2. Of those that a mesh axis runs over, the one named last changes fastest.
Arguments:
- counts: bfloat16 [128, 65536], P(None, ('grp', 'peak')), may hold values from 0.099609375 to 4
- tile_mask: int32 [128, 512], P(None, ('grp', 'peak')), may hold values 0 or 1
- neighbours: int32 [128, 15], P(('grp', 'peak')), may hold values from 0 to 127, as said below
- peak_weight: bfloat16 [65536, 512], P(('grp', 'peak')), may hold values from -0.0390625 to 0.0390625
- gain: float32 [512], replicated, may hold values from 0.25 to 1.75
- w_in: bfloat16 [512, 512], replicated, may hold values from -0.25 to 0.25
- w_out: bfloat16 [512, 256], replicated, may hold values from -0.25 to 0.25
Outputs:
- peak_grad: float32 [65536, 512], P(('grp', 'peak'))
- gain_grad: float32 [512], replicated
- in_grad: float32 [512, 512], replicated
- out_grad: float32 [512, 256], replicated
The draws below stay inside these ranges and needn't reach their ends.
Inputs may be any that keep to these rules, and one draw needn't show every extreme that they name: `neighbours`: every entry is a cell index other than its own row's cell.
All inputs are finite; a program needn't handle non-finite values. No bound on the sum of `tile_mask` on one device may be relied on, other than what follows from the above.
Results may differ from the reference program's by a relative error of at most 0.012.
Values may be sent and summed in bfloat16 or wider, within the bound.
No kernel may reach another device: no remote copies, remote signals or barrier semaphores. Data moves between devices by JAX's collectives and lax.ppermute only.
A program may use at most 64 MiB of HBM per device.

```python
import math
import jax
import jax.numpy as jnp
from jax import lax

D = 512
HID = 512
E = 256
TILE = 128
K = 15
CELLS = 128
PEAKS = 65536
TILES = 512


def draw_neighbours(key, part):
    offsets = jax.random.randint(key, (CELLS, K), 1, CELLS)
    base_rows = jnp.arange(CELLS, dtype=jnp.int32)[:, None]
    return ((base_rows + offsets) % CELLS).astype(jnp.int32)


def set_ends(values, key, smallest, top_value):
    longest = values.shape.index(max(values.shape))
    spots = []
    for shift in (0, 1):
        where = [jax.random.randint(jax.random.fold_in(key, axis), (), 0, length) for axis, length in enumerate(values.shape)]
        where[longest] = (where[longest] + shift) % values.shape[longest]
        spots.append(tuple(where))
    return values.at[spots[0]].set(smallest).at[spots[1]].set(top_value)


def levels(stream_key, shape, shards, smallest, largest):
    level = 1.0
    for dim, shards_of in shards:
        heights = jax.random.uniform(jax.random.fold_in(jax.random.fold_in(stream_key, 6), dim), (shards_of,), jnp.float32, smallest / len(shards), largest / len(shards))
        level = level * jnp.repeat(jnp.exp(heights), shape[dim] // shards_of).reshape((-1,) + (1,) * (len(shape) - 1 - dim))
    return level


def scatter_about(key, extent, spread, bound, split=(), kind=jnp.bfloat16):
    factor_of = levels(key, extent, split, -0.22, 0.18) if split else 1.0
    entries = jax.random.normal(key, extent, jnp.float32) * spread * factor_of
    return jnp.minimum(jnp.maximum(entries, -bound), bound).astype(kind)


def setup_inputs(seed: int = 0) -> dict:
    key_list = jax.random.split(jax.random.key(seed), 8)
    return {
        "counts": jnp.clip(jnp.exp(math.log(4.0) - 3.6927934 * jax.random.uniform(key_list[0], (CELLS, PEAKS), jnp.float32) ** levels(key_list[0], (CELLS, PEAKS), ((1, 32),), -0.2, 0.2)), 0.099609375, 4.0).astype(jnp.bfloat16),
        "tile_mask": set_ends((jax.random.randint(key_list[1], (CELLS, TILES), 0, 3) < 1).astype(jnp.int32), jax.random.fold_in(key_list[1], 1), 0, 1),
        "neighbours": draw_neighbours(jax.random.fold_in(key_list[7], 71), 0),
        "peak_weight": scatter_about(key_list[3], (PEAKS, D), (PEAKS // 3) ** -0.5, 0.0390625, ((0, 32),)),
        "gain": jnp.clip(1.0 + 0.15 * jax.random.normal(key_list[4], (D,), jnp.float32), 0.25, 1.75),
        "w_in": scatter_about(key_list[5], (D, HID), D ** -0.5, 0.25),
        "w_out": scatter_about(key_list[6], (HID, E), HID ** -0.5, 0.25),
    }


sharpness_divisor = 0.2
eps_norm = 1e-06
gelu_coef = 0.7978845608
cubic_coef = 0.044715

def gelu_tanh(values):
    return 0.5 * values * (1.0 + jnp.tanh(gelu_coef * (values + cubic_coef * values * values * values)))

def gelu_slope(values):
    tangent = jnp.tanh(gelu_coef * (values + cubic_coef * values * values * values))
    return 0.5 * (1.0 + tangent) + 0.5 * values * (1.0 - tangent * tangent) * gelu_coef * (1.0 + 3.0 * cubic_coef * values * values)

def collapsed_lines(left, right):
    return lax.dot_general(left, right, (((0,), (0,)), ((), ())), preferred_element_type=jnp.float32)

def tower_forward(hidden, gain, w_in, w_out):
    scale = lax.rsqrt(lax.optimization_barrier(jnp.mean(hidden * hidden, axis=1, keepdims=True)) + eps_norm)
    normed = hidden * scale
    rounded = (normed * gain[None, :]).astype(jnp.bfloat16)
    preact = jnp.dot(rounded, w_in, preferred_element_type=jnp.float32)
    activ = gelu_tanh(preact).astype(jnp.bfloat16)
    project = jnp.dot(activ, w_out, preferred_element_type=jnp.float32)
    length = lax.rsqrt(lax.optimization_barrier(jnp.sum(project * project, axis=1, keepdims=True)) + eps_norm)
    unit = project * length
    return ((scale, normed, rounded, preact, activ, length, unit), unit.astype(jnp.bfloat16))

def tower_backward(vector_derivative, gain, w_in, w_out, saved):
    scale, normed, rounded, preact, activ, length, unit = saved
    dproj = (length * (vector_derivative - unit * lax.optimization_barrier(jnp.sum(unit * vector_derivative, axis=1, keepdims=True)))).astype(jnp.bfloat16)
    out_grad = collapsed_lines(activ, dproj)
    dact = jnp.dot(dproj, w_out.T, preferred_element_type=jnp.float32)
    dpre = (dact * gelu_slope(preact)).astype(jnp.bfloat16)
    in_grad = collapsed_lines(rounded, dpre)
    dround = jnp.dot(dpre, w_in.T, preferred_element_type=jnp.float32)
    gain_grad = lax.optimization_barrier(jnp.sum(dround * normed, axis=0))
    dnorm = dround * gain[None, :]
    dhidden = scale * (dnorm - normed * lax.optimization_barrier(jnp.mean(dnorm * normed, axis=1, keepdims=True)))
    return (dhidden.astype(jnp.bfloat16), gain_grad, in_grad, out_grad)

def reference(counts, tile_mask, neighbours, peak_weight, gain, w_in, w_out):
    masked = counts * jnp.repeat(tile_mask.astype(jnp.bfloat16), TILE, axis=1)
    hidden = jnp.dot(masked, peak_weight, preferred_element_type=jnp.float32)
    saved, sample_vectors = tower_forward(hidden, gain, w_in, w_out)
    affinity_scores = jnp.dot(sample_vectors, sample_vectors.T, preferred_element_type=jnp.float32) / sharpness_divisor
    rows = lax.broadcasted_iota(jnp.int32, (CELLS, CELLS), 0)
    cols = lax.broadcasted_iota(jnp.int32, (CELLS, CELLS), 1)
    expo = jnp.where(rows == cols, jnp.float32(0.0), jnp.exp(affinity_scores))
    prob = expo / lax.optimization_barrier(jnp.sum(expo, axis=1, keepdims=True))
    tallies = jnp.zeros((CELLS, CELLS), jnp.float32)
    for slot in range(K):
        tallies = tallies + (neighbours[:, slot][:, None] == cols).astype(jnp.float32)
    neighbour_coefficients = (prob - tallies / K).astype(jnp.bfloat16)
    vector_derivative = (jnp.dot(neighbour_coefficients, sample_vectors, preferred_element_type=jnp.float32) + collapsed_lines(neighbour_coefficients, sample_vectors)) / sharpness_divisor
    dhidden, gain_grad, in_grad, out_grad = tower_backward(vector_derivative, gain, w_in, w_out, saved)
    peak_grad = collapsed_lines(masked, dhidden)
    return (peak_grad, gain_grad, in_grad, out_grad)
```

```python
import functools

import jax
import jax.numpy as jnp
from jax import lax
from jax.experimental import pallas as pl
from jax.experimental.pallas import tpu as pltpu
from jax.sharding import PartitionSpec as P

TILE = 128
EXTRA = 16
ALL = ("grp", "peak")
VMEM_BYTES = 56 * 1024 * 1024

sharpness_divisor = 0.2
eps_norm = 1e-06
gelu_coef = 0.7978845608
cubic_coef = 0.044715

F32 = jnp.float32
BF16 = jnp.bfloat16


def dot(left, right, left_dim, right_dim):
    return lax.dot_general(
        left, right, (((left_dim,), (right_dim,)), ((), ())), preferred_element_type=F32
    )


def core_index():
    return lax.rem(lax.axis_index("grp"), 2)


def partial_kernel(
    carried, pieces, counts_hbm, mask_ref, lists_ref, weight_hbm, send_ref, keep_ref,
    counts_ref, weight_ref, total_ref, counts_sem, weight_sem,
):
    cells, peaks = counts_ref.shape
    half = cells // 2
    span = peaks // pieces

    def copies(piece):
        at = pl.ds(piece * span, span)
        return (
            pltpu.make_async_copy(counts_hbm.at[:, at], counts_ref.at[:, at], counts_sem.at[piece]),
            pltpu.make_async_copy(weight_hbm.at[at, :], weight_ref.at[at, :], weight_sem.at[piece]),
        )

    for piece in range(pieces):
        for copy in copies(piece):
            copy.start()
    mask = mask_ref[...].astype(F32).astype(BF16)
    for piece in range(pieces):
        for copy in copies(piece):
            copy.wait()
        first = piece * span
        masked = jnp.concatenate(
            [
                counts_ref[:, start : start + TILE] * mask[:, start // TILE : start // TILE + 1]
                for start in range(first, first + span, TILE)
            ],
            axis=1,
        )
        term = jnp.dot(masked, weight_ref[first : first + span, :], preferred_element_type=F32)
        total_ref[...] = term if piece == 0 else total_ref[...] + term
    core = core_index()
    send_ref[:half, :] = total_ref[pl.ds((1 - core) * half, half), :].astype(BF16)
    keep_ref[:half, :] = total_ref[pl.ds(core * half, half), :].astype(BF16)
    if carried:
        own, length = lists_ref.shape
        position = lax.axis_index("grp") * lax.axis_size("peak") + lax.axis_index("peak")
        columns = lax.broadcasted_iota(jnp.int32, (own, keep_ref.shape[1]), 1)
        rows = lax.broadcasted_iota(jnp.int32, (own, keep_ref.shape[1]), 0)
        place = (columns == rows + position * own).astype(F32)
        lists = dot(lists_ref[...].astype(F32), place, 0, 0)
        lists = jnp.concatenate([lists, jnp.zeros((2 * EXTRA - length, lists.shape[1]), F32)], axis=0)
        low, high = lists[:EXTRA], lists[EXTRA:]
        send_ref[half:, :] = jnp.where(core == 0, high, low).astype(BF16)
        keep_ref[half:, :] = jnp.where(core == 0, low, high).astype(BF16)


def partial_hidden(carried, counts, tile_mask, neighbours, peak_weight):
    cells, peaks = counts.shape
    width = peak_weight.shape[1]
    pieces = 4
    whole = pl.BlockSpec(memory_space=pltpu.VMEM)
    remote = pl.BlockSpec(memory_space=pl.ANY)
    rows = cells // 2 + (EXTRA if carried else 0)
    return pl.pallas_call(
        functools.partial(partial_kernel, carried, pieces),
        out_shape=[jax.ShapeDtypeStruct((rows, width), BF16)] * 2,
        in_specs=[remote, whole, whole, remote],
        out_specs=[whole, whole],
        scratch_shapes=[
            pltpu.VMEM((cells, peaks), BF16),
            pltpu.VMEM((peaks, width), BF16),
            pltpu.VMEM((cells, width), F32),
            pltpu.SemaphoreType.DMA((pieces,)),
            pltpu.SemaphoreType.DMA((pieces,)),
        ],
        compiler_params=pltpu.CompilerParams(vmem_limit_bytes=VMEM_BYTES),
        cost_estimate=pl.CostEstimate(
            flops=2 * cells * peaks * width,
            bytes_accessed=2 * (cells * peaks + peaks * width + 2 * rows * width),
            transcendentals=0,
        ),
    )(counts, tile_mask, neighbours, peak_weight)


def turn_kernel(counts_ref, mask_ref, turned_ref):
    mask = mask_ref[...].astype(F32).astype(BF16)
    for start in range(0, counts_ref.shape[1], TILE):
        tile = start // TILE
        piece = counts_ref[:, start : start + TILE] * mask[:, tile : tile + 1]
        turned_ref[start : start + TILE, :] = piece.T


def turn(counts, tile_mask):
    cells, peaks = counts.shape
    whole = pl.BlockSpec(memory_space=pltpu.VMEM)
    return pl.pallas_call(
        turn_kernel,
        out_shape=jax.ShapeDtypeStruct((peaks, cells), BF16),
        in_specs=[whole, whole],
        out_specs=whole,
        compiler_params=pltpu.CompilerParams(vmem_limit_bytes=VMEM_BYTES),
        cost_estimate=pl.CostEstimate(
            flops=cells * peaks, bytes_accessed=4 * cells * peaks, transcendentals=0
        ),
    )(counts, tile_mask)


def tower_kernel(
    carried, length_of, pieces, own_ref, other_ref, lists_ref, turned_ref, gain_ref, w_in_ref, w_out_ref,
    peak_grad_hbm, gain_grad_ref, in_grad_hbm, out_grad_hbm,
    hidden_ref, peak_grad_ref, in_grad_ref, out_grad_ref, peak_sem, side_sem,
):
    cells = hidden_ref.shape[0]
    half = cells // 2
    core = core_index()
    hidden_ref[pl.ds(core * half, half), :] = own_ref[:half, :].astype(F32)
    hidden_ref[pl.ds((1 - core) * half, half), :] = other_ref[:half, :].astype(F32)
    if carried:
        own_lists, other_lists = own_ref[half:, :cells].astype(F32), other_ref[half:, :cells].astype(F32)
        lists = jnp.concatenate(
            [jnp.where(core == 0, own_lists, other_lists), jnp.where(core == 0, other_lists, own_lists)], axis=0
        )
    else:
        lists = lists_ref[...].astype(F32)
    gain = gain_ref[...]
    w_in, w_out = w_in_ref[...], w_out_ref[...]

    hidden = hidden_ref[...]
    scale = lax.rsqrt(jnp.mean(hidden * hidden, axis=1, keepdims=True) + eps_norm)
    normed = hidden * scale
    rounded = (normed * gain).astype(BF16)
    preact = jnp.dot(rounded, w_in, preferred_element_type=F32)
    square = preact * preact
    tangent = jnp.tanh(gelu_coef * preact * (1.0 + cubic_coef * square))
    activ = (0.5 * preact * (1.0 + tangent)).astype(BF16)
    slope = 0.5 * (1.0 + tangent) + 0.5 * preact * (1.0 - tangent * tangent) * gelu_coef * (
        1.0 + 3.0 * cubic_coef * square
    )
    project = jnp.dot(activ, w_out, preferred_element_type=F32)
    length = lax.rsqrt(jnp.sum(project * project, axis=1, keepdims=True) + eps_norm)
    unit = project * length
    codes = unit.astype(BF16)

    scores = dot(codes, codes, 1, 1) / sharpness_divisor
    targets = lax.broadcasted_iota(jnp.int32, (cells, cells), 0)
    sources = lax.broadcasted_iota(jnp.int32, (cells, cells), 1)
    expo = jnp.where(targets == sources, 0.0, jnp.exp(scores))
    prob = expo * (1.0 / jnp.sum(expo, axis=0, keepdims=True))
    places = targets.astype(F32)
    tallies = jnp.zeros((cells, cells), F32)
    for slot in range(length_of):
        tallies = tallies + (lists[slot : slot + 1, :] == places).astype(F32)
    coupling = (prob - tallies / length_of).astype(BF16)
    dcodes = (dot(coupling, codes, 0, 0) + dot(coupling, codes, 1, 0)) / sharpness_divisor

    dproj = (length * (dcodes - unit * jnp.sum(unit * dcodes, axis=1, keepdims=True))).astype(BF16)
    dpre = (dot(dproj, w_out, 1, 1) * slope).astype(BF16)
    dround = dot(dpre, w_in, 1, 1)
    gain_grad_ref[...] = jnp.sum(dround * normed, axis=0, keepdims=True)
    dnorm = dround * gain
    dhidden = (scale * (dnorm - normed * jnp.mean(dnorm * normed, axis=1, keepdims=True))).astype(BF16)

    span = turned_ref.shape[0] // pieces

    def peak_copy(piece):
        at = pl.ds(piece * span, span)
        return pltpu.make_async_copy(peak_grad_ref.at[at, :], peak_grad_hbm.at[at, :], peak_sem.at[piece])

    for piece in range(pieces):
        at = pl.ds(piece * span, span)
        peak_grad_ref[at, :] = jnp.dot(turned_ref[at, :], dhidden, preferred_element_type=F32)
        peak_copy(piece).start()
    in_copy = pltpu.make_async_copy(in_grad_ref, in_grad_hbm, side_sem.at[0])
    out_copy = pltpu.make_async_copy(out_grad_ref, out_grad_hbm, side_sem.at[1])
    in_grad_ref[...] = dot(rounded, dpre, 0, 0)
    in_copy.start()
    out_grad_ref[...] = dot(activ, dproj, 0, 0)
    out_copy.start()
    for piece in range(pieces):
        peak_copy(piece).wait()
    in_copy.wait()
    out_copy.wait()


def tower(carried, length_of, own, other, lists, turned, gain, w_in, w_out):
    peaks, cells = turned.shape
    width, hid = w_in.shape
    codes = w_out.shape[1]
    pieces = 8
    whole = pl.BlockSpec(memory_space=pltpu.VMEM)
    remote = pl.BlockSpec(memory_space=pl.ANY)
    return pl.pallas_call(
        functools.partial(tower_kernel, carried, length_of, pieces),
        out_shape=[
            jax.ShapeDtypeStruct((peaks, width), F32),
            jax.ShapeDtypeStruct((1, width), F32),
            jax.ShapeDtypeStruct((width, hid), F32),
            jax.ShapeDtypeStruct((hid, codes), F32),
        ],
        in_specs=[whole] * 7,
        out_specs=[remote, whole, remote, remote],
        scratch_shapes=[
            pltpu.VMEM((cells, width), F32),
            pltpu.VMEM((peaks, width), F32),
            pltpu.VMEM((width, hid), F32),
            pltpu.VMEM((hid, codes), F32),
            pltpu.SemaphoreType.DMA((pieces,)),
            pltpu.SemaphoreType.DMA((2,)),
        ],
        compiler_params=pltpu.CompilerParams(vmem_limit_bytes=VMEM_BYTES),
        cost_estimate=pl.CostEstimate(
            flops=2 * cells * width * (peaks + 3 * hid + 3 * codes),
            bytes_accessed=2 * peaks * cells + 4 * peaks * width + 6 * width * hid + 6 * hid * codes,
            transcendentals=cells * (hid + cells),
        ),
    )(own, other, lists, turned, gain, w_in, w_out)


def flips(n_grp, n_peak):
    grp_bits = [bit * n_peak for bit in (2, 4, 8, 16, 32, 64) if bit < n_grp]
    peak_bits = [bit for bit in (1, 2, 4, 8, 16, 32, 64) if bit < n_peak]
    order = grp_bits + peak_bits
    if len(order) == 4:
        order = [order[0], order[2], order[1], order[3]]
    swapped = list(order)
    for at in range(0, len(order) - 1, 2):
        swapped[at], swapped[at + 1] = order[at + 1], order[at]
    return list(zip(order, swapped, strict=True))


def body(n_grp, n_peak, counts, tile_mask, neighbours, peak_weight, gain, w_in, w_out):
    cells = counts.shape[0]
    length_of = neighbours.shape[1]
    carried = cells <= 256 and cells <= peak_weight.shape[1]
    devices = n_grp * n_peak

    def exchange(values, bits):
        pairs = [(i, i ^ bits[(i // n_peak) % 2]) for i in range(devices)]
        return lax.ppermute(values, ALL, pairs)

    def add(left, right):
        return (left.astype(F32) + right.astype(F32)).astype(BF16)

    send, held = partial_hidden(carried, counts, tile_mask, neighbours, peak_weight)
    held = add(held, exchange(send, (n_peak, n_peak)))
    turned = turn(counts, tile_mask)
    for bits in flips(n_grp, n_peak):
        held = add(held, exchange(held, bits))
    other = exchange(held, (n_peak, n_peak))
    if carried:
        lists = neighbours
    else:
        lists = lax.all_gather(neighbours, ALL, axis=0, tiled=True).T
    peak_grad, gain_grad, in_grad, out_grad = tower(
        carried, length_of, held, other, lists, turned, gain.reshape(1, -1), w_in, w_out
    )
    return (peak_grad, gain_grad.reshape(-1), in_grad, out_grad)


def solution(mesh):
    placed = (
        P(None, ALL),
        P(None, ALL),
        P(ALL, None),
        P(ALL, None),
        P(),
        P(),
        P(),
    )
    return jax.shard_map(
        functools.partial(body, mesh.shape["grp"], mesh.shape["peak"]),
        mesh=mesh,
        in_specs=placed,
        out_specs=(P(ALL, None), P(), P(), P()),
        check_vma=False,
    )
```

```python
import functools

import jax
import jax.numpy as jnp
from jax import lax
from jax.experimental import pallas as pl
from jax.experimental.pallas import tpu as pltpu
from jax.sharding import PartitionSpec as P

TILE = 128
EXTRA = 16
ALL = ("grp", "peak")
MIB = 1024 * 1024
F32 = jnp.float32
BF16 = jnp.bfloat16
LINK = jnp.float16
LIFT = 2.0

sharpness_divisor = 0.2
eps_norm = 1e-06
gelu_coef = 0.7978845608
cubic_coef = 0.044715


def dot(left, right, left_dim, right_dim):
    return lax.dot_general(
        left, right, (((left_dim,), (right_dim,)), ((), ())), preferred_element_type=F32
    )


def core_index():
    return lax.rem(lax.axis_index("grp"), 2)


def partial_kernel(
    carried, pieces, counts_hbm, mask_hbm, lists_hbm, weight_hbm, send_ref, keep_ref,
    counts_ref, mask_ref, lists_ref, weight_ref, total_ref, counts_sem, weight_sem, side_sem,
):
    cells, peaks = counts_ref.shape
    half = cells // 2
    span = peaks // pieces

    def copies(piece):
        at = pl.ds(piece * span, span)
        return (
            pltpu.make_async_copy(counts_hbm.at[:, at], counts_ref.at[:, at], counts_sem.at[piece]),
            pltpu.make_async_copy(weight_hbm.at[at, :], weight_ref.at[at, :], weight_sem.at[piece]),
        )

    sides = (
        pltpu.make_async_copy(mask_hbm, mask_ref, side_sem.at[0]),
        pltpu.make_async_copy(lists_hbm, lists_ref, side_sem.at[1]),
    )
    for copy in sides:
        copy.start()
    for piece in range(pieces):
        for copy in copies(piece):
            copy.start()
    for copy in sides:
        copy.wait()
    core = core_index()
    if carried:
        own, length = lists_ref.shape
        position = lax.axis_index("grp") * lax.axis_size("peak") + lax.axis_index("peak")
        columns = lax.broadcasted_iota(jnp.int32, (own, keep_ref.shape[1]), 1)
        rows = lax.broadcasted_iota(jnp.int32, (own, keep_ref.shape[1]), 0)
        place = (columns == rows + position * own).astype(F32)
        lists = dot(lists_ref[...].astype(F32), place, 0, 0)
        lists = jnp.concatenate([lists, jnp.zeros((2 * EXTRA - length, lists.shape[1]), F32)], axis=0)
        low, high = lists[:EXTRA], lists[EXTRA:]
        send_ref[half:, :] = jnp.where(core == 0, high, low)
        keep_ref[half:, :] = jnp.where(core == 0, low, high)
    mask = (LIFT * mask_ref[...].astype(F32)).T
    for piece in range(pieces):
        for copy in copies(piece):
            copy.wait()
        first = piece * span
        masked = jnp.concatenate(
            [
                counts_ref[:, start : start + TILE]
                * jnp.broadcast_to(mask[:, start // TILE : start // TILE + 1], (cells, TILE)).astype(BF16)
                for start in range(first, first + span, TILE)
            ],
            axis=1,
        )
        term = jnp.dot(masked, weight_ref[first : first + span, :], preferred_element_type=F32)
        total_ref[...] = term if piece == 0 else total_ref[...] + term
    send_ref[:half, :] = total_ref[pl.ds((1 - core) * half, half), :]
    keep_ref[:half, :] = total_ref[pl.ds(core * half, half), :]


def partial_hidden(carried, counts, mask, neighbours, peak_weight):
    cells, peaks = counts.shape
    width = peak_weight.shape[1]
    pieces = 4
    whole = pl.BlockSpec(memory_space=pltpu.VMEM)
    main = pl.BlockSpec(memory_space=pltpu.HBM)
    rows = cells // 2 + (EXTRA if carried else 0)
    return pl.pallas_call(
        functools.partial(partial_kernel, carried, pieces),
        out_shape=[pltpu.VMEM((rows, width), F32)] * 2,
        in_specs=[main] * 4,
        out_specs=[whole, whole],
        scratch_shapes=[
            pltpu.VMEM((cells, peaks), BF16),
            pltpu.VMEM(mask.shape, jnp.int32),
            pltpu.VMEM(neighbours.shape, jnp.int32),
            pltpu.VMEM((peaks, width), BF16),
            pltpu.VMEM((cells, width), F32),
            pltpu.SemaphoreType.DMA((pieces,)),
            pltpu.SemaphoreType.DMA((pieces,)),
            pltpu.SemaphoreType.DMA((2,)),
        ],
        compiler_params=pltpu.CompilerParams(
            vmem_limit_bytes=4 * MIB + 2 * (cells * peaks + peaks * width) + 20 * cells * width
        ),
        cost_estimate=pl.CostEstimate(
            flops=2 * cells * peaks * width,
            bytes_accessed=2 * (cells * peaks + peaks * width) + 8 * rows * width,
            transcendentals=0,
        ),
    )(*(pltpu.with_memory_space_constraint(x, pltpu.HBM) for x in (counts, mask, neighbours, peak_weight)))


def turn_kernel(counts_ref, mask_ref, turned_ref):
    cells = counts_ref.shape[0]
    mask = mask_ref[...].astype(F32).T
    for start in range(0, counts_ref.shape[1], TILE):
        tile = start // TILE
        column = jnp.broadcast_to(mask[:, tile : tile + 1], (cells, TILE)).astype(BF16)
        turned_ref[start : start + TILE, :] = (counts_ref[:, start : start + TILE] * column).T


def turn(counts, mask):
    cells, peaks = counts.shape
    whole = pl.BlockSpec(memory_space=pltpu.VMEM)
    return pl.pallas_call(
        turn_kernel,
        out_shape=jax.ShapeDtypeStruct((peaks, cells), BF16),
        in_specs=[whole, whole],
        out_specs=whole,
        compiler_params=pltpu.CompilerParams(vmem_limit_bytes=4 * MIB + 8 * cells * peaks),
        cost_estimate=pl.CostEstimate(
            flops=cells * peaks, bytes_accessed=4 * cells * peaks, transcendentals=0
        ),
    )(counts, mask)


def tower_kernel(
    carried, length_of, pieces, own_ref, other_ref, lists_ref, turned_ref, gain_ref, w_in_ref, w_out_ref,
    peak_grad_hbm, gain_grad_ref, in_grad_hbm, out_grad_hbm,
    hidden_ref, peak_grad_ref, in_grad_ref, out_grad_ref, peak_sem, side_sem,
):
    cells = hidden_ref.shape[0]
    half = cells // 2
    core = core_index()
    hidden_ref[pl.ds(core * half, half), :] = own_ref[:half, :] * (1.0 / LIFT)
    hidden_ref[pl.ds((1 - core) * half, half), :] = other_ref[:half, :] * (1.0 / LIFT)
    if carried:
        own_lists, other_lists = own_ref[half:, :cells], other_ref[half:, :cells]
        lists = jnp.concatenate(
            [jnp.where(core == 0, own_lists, other_lists), jnp.where(core == 0, other_lists, own_lists)], axis=0
        )
    else:
        lists = lists_ref[...].astype(F32)
    gain = gain_ref[...]
    w_in, w_out = w_in_ref[...], w_out_ref[...]

    hidden = hidden_ref[...]
    scale = lax.rsqrt(jnp.mean(hidden * hidden, axis=1, keepdims=True) + eps_norm)
    normed = hidden * scale
    rounded = (normed * gain).astype(BF16)
    preact = jnp.dot(rounded, w_in, preferred_element_type=F32)
    square = preact * preact
    tangent = jnp.tanh(gelu_coef * preact * (1.0 + cubic_coef * square))
    activ = (0.5 * preact * (1.0 + tangent)).astype(BF16)
    slope = 0.5 * (1.0 + tangent) + 0.5 * preact * (1.0 - tangent * tangent) * gelu_coef * (
        1.0 + 3.0 * cubic_coef * square
    )
    project = jnp.dot(activ, w_out, preferred_element_type=F32)
    length = lax.rsqrt(jnp.sum(project * project, axis=1, keepdims=True) + eps_norm)
    unit = project * length
    codes = unit.astype(BF16)

    scores = dot(codes, codes, 1, 1) / sharpness_divisor
    targets = lax.broadcasted_iota(jnp.int32, (cells, cells), 0)
    sources = lax.broadcasted_iota(jnp.int32, (cells, cells), 1)
    expo = jnp.where(targets == sources, 0.0, jnp.exp(scores))
    prob = expo * (1.0 / jnp.sum(expo, axis=0, keepdims=True))
    places = targets.astype(F32)
    tallies = jnp.zeros((cells, cells), F32)
    for slot in range(length_of):
        tallies = tallies + (lists[slot : slot + 1, :] == places).astype(F32)
    coupling = (prob - tallies / length_of).astype(BF16)
    dcodes = (dot(coupling, codes, 0, 0) + dot(coupling, codes, 1, 0)) / sharpness_divisor

    dproj = (length * (dcodes - unit * jnp.sum(unit * dcodes, axis=1, keepdims=True))).astype(BF16)
    dpre = (dot(dproj, w_out, 1, 1) * slope).astype(BF16)
    dround = dot(dpre, w_in, 1, 1)
    gain_grad_ref[...] = jnp.sum(dround * normed, axis=0, keepdims=True)
    dnorm = dround * gain
    dhidden = (scale * (dnorm - normed * jnp.mean(dnorm * normed, axis=1, keepdims=True))).astype(BF16)

    span = turned_ref.shape[0] // pieces

    def peak_copy(piece):
        at = pl.ds(piece * span, span)
        return pltpu.make_async_copy(peak_grad_ref.at[at, :], peak_grad_hbm.at[at, :], peak_sem.at[piece])

    for piece in range(pieces):
        at = pl.ds(piece * span, span)
        peak_grad_ref[at, :] = jnp.dot(turned_ref[at, :], dhidden, preferred_element_type=F32)
        peak_copy(piece).start()
    in_copy = pltpu.make_async_copy(in_grad_ref, in_grad_hbm, side_sem.at[0])
    out_copy = pltpu.make_async_copy(out_grad_ref, out_grad_hbm, side_sem.at[1])
    in_grad_ref[...] = dot(rounded, dpre, 0, 0)
    in_copy.start()
    out_grad_ref[...] = dot(activ, dproj, 0, 0)
    out_copy.start()
    for piece in range(pieces):
        peak_copy(piece).wait()
    in_copy.wait()
    out_copy.wait()


def tower(carried, length_of, own, other, lists, turned, gain, w_in, w_out):
    peaks, cells = turned.shape
    width, hid = w_in.shape
    codes = w_out.shape[1]
    pieces = 8
    whole = pl.BlockSpec(memory_space=pltpu.VMEM)
    main = pl.BlockSpec(memory_space=pltpu.HBM)
    return pl.pallas_call(
        functools.partial(tower_kernel, carried, length_of, pieces),
        out_shape=[
            jax.ShapeDtypeStruct((peaks, width), F32),
            jax.ShapeDtypeStruct((1, width), F32),
            jax.ShapeDtypeStruct((width, hid), F32),
            jax.ShapeDtypeStruct((hid, codes), F32),
        ],
        in_specs=[whole] * 7,
        out_specs=[main, whole, main, main],
        scratch_shapes=[
            pltpu.VMEM((cells, width), F32),
            pltpu.VMEM((peaks, width), F32),
            pltpu.VMEM((width, hid), F32),
            pltpu.VMEM((hid, codes), F32),
            pltpu.SemaphoreType.DMA((pieces,)),
            pltpu.SemaphoreType.DMA((2,)),
        ],
        compiler_params=pltpu.CompilerParams(
            vmem_limit_bytes=min(
                56 * MIB,
                4 * (MIB + peaks * width + width * hid + hid * codes) + cells * (64 * width + 20 * cells),
            )
        ),
        cost_estimate=pl.CostEstimate(
            flops=2 * cells * width * (peaks + 3 * hid + 3 * codes),
            bytes_accessed=2 * peaks * cells + 4 * peaks * width + 6 * width * hid + 6 * hid * codes,
            transcendentals=cells * (hid + cells),
        ),
    )(own, other, lists, turned, gain, w_in, w_out)


def flips(n_grp, n_peak):
    grp_bits = [bit * n_peak for bit in (2, 4, 8, 16, 32, 64) if bit < n_grp]
    peak_bits = [bit for bit in (1, 2, 4, 8, 16, 32, 64) if bit < n_peak]
    order = grp_bits + peak_bits
    if len(order) == 4:
        order = [order[0], order[2], order[1], order[3]]
    swapped = list(order)
    for at in range(0, len(order) - 1, 2):
        swapped[at], swapped[at + 1] = order[at + 1], order[at]
    return list(zip(order, swapped, strict=True))


def body(n_grp, n_peak, counts, tile_mask, neighbours, peak_weight, gain, w_in, w_out):
    cells = counts.shape[0]
    length_of = neighbours.shape[1]
    carried = cells <= 256 and cells <= peak_weight.shape[1]
    devices = n_grp * n_peak

    def exchange(values, bits):
        pairs = [(i, i ^ bits[(i // n_peak) % 2]) for i in range(devices)]
        return lax.ppermute(values, ALL, pairs)

    def add(left, right):
        return lax.optimization_barrier((left.astype(F32) + right.astype(F32)).astype(LINK))

    mask = tile_mask.T
    send, held = partial_hidden(carried, counts, mask, neighbours, peak_weight)
    held = add(held, exchange(send, (n_peak, n_peak)))
    turned = turn(counts, mask)
    steps = flips(n_grp, n_peak)
    for at, bits in enumerate(steps):
        held = add(held, exchange(held, bits))
        if at == len(steps) // 2:
            held, turned = lax.optimization_barrier((held, turned))
    other = exchange(held, (n_peak, n_peak)).astype(F32)
    held = held.astype(F32)
    if carried:
        lists = neighbours
    else:
        lists = lax.all_gather(neighbours, ALL, axis=0, tiled=True).T
    peak_grad, gain_grad, in_grad, out_grad = tower(
        carried, length_of, held, other, lists, turned, gain.reshape(1, -1), w_in, w_out
    )
    return (peak_grad, gain_grad.reshape(-1), in_grad, out_grad)


def solution(mesh):
    placed = (
        P(None, ALL),
        P(None, ALL),
        P(ALL, None),
        P(ALL, None),
        P(),
        P(),
        P(),
    )
    return jax.shard_map(
        functools.partial(body, mesh.shape["grp"], mesh.shape["peak"]),
        mesh=mesh,
        in_specs=placed,
        out_specs=(P(ALL, None), P(), P(), P()),
        check_vma=False,
    )
```

```python
import functools

import jax
import jax.numpy as jnp
from jax import lax
from jax.experimental import pallas as pl
from jax.experimental.pallas import tpu as pltpu
from jax.sharding import PartitionSpec as P

TILE = 128
EXTRA = 8
ALL = ("grp", "peak")
MIB = 1024 * 1024
F32 = jnp.float32
BF16 = jnp.bfloat16
LINK = jnp.float16
LIFT = 2.0

sharpness_divisor = 0.2
eps_norm = 1e-06
gelu_coef = 0.7978845608
cubic_coef = 0.044715


def dot(left, right, left_dim, right_dim):
    return lax.dot_general(
        left, right, (((left_dim,), (right_dim,)), ((), ())), preferred_element_type=F32
    )


def place():
    return lax.axis_index("grp") * lax.axis_size("peak") + lax.axis_index("peak")


def own_half():
    position = place()
    ones = position
    for bit in range(1, (lax.axis_size("grp") * lax.axis_size("peak")).bit_length()):
        ones = ones + lax.shift_right_logical(position, bit)
    return lax.rem(ones, 2)


def list_places(length, cells, width):
    half = -(-length // 2)
    across = width // cells
    return [(slot // half, slot % half // across, slot % half % across * cells) for slot in range(length)]


def partial_kernel(
    carried, pieces, counts_hbm, mask_hbm, lists_hbm, weight_hbm, send_ref, keep_ref, masked_ref,
    counts_ref, mask_ref, lists_ref, weight_ref, total_ref, counts_sem, weight_sem, side_sem,
):
    cells, peaks = counts_ref.shape
    half = cells // 2
    span = peaks // pieces

    def copies(piece):
        at = pl.ds(piece * span, span)
        return (
            pltpu.make_async_copy(counts_hbm.at[:, at], counts_ref.at[:, at], counts_sem.at[piece]),
            pltpu.make_async_copy(weight_hbm.at[at, :], weight_ref.at[at, :], weight_sem.at[piece]),
        )

    sides = (
        pltpu.make_async_copy(mask_hbm, mask_ref, side_sem.at[0]),
        pltpu.make_async_copy(lists_hbm, lists_ref, side_sem.at[1]),
    )
    for copy in sides:
        copy.start()
    for piece in range(pieces):
        for copy in copies(piece):
            copy.start()
    for copy in sides:
        copy.wait()
    mine = own_half()
    if carried:
        own, length = lists_ref.shape
        columns = lax.broadcasted_iota(jnp.int32, (own, cells), 1)
        rows = lax.broadcasted_iota(jnp.int32, (own, cells), 0)
        lists = dot(lists_ref[...].astype(F32), (columns == rows + place() * own).astype(F32), 0, 0)
        send_ref[half:, :] = jnp.zeros((EXTRA, send_ref.shape[1]), F32)
        keep_ref[half:, :] = jnp.zeros((EXTRA, keep_ref.shape[1]), F32)
        for slot, (side, row, column) in enumerate(list_places(length, cells, keep_ref.shape[1])):
            at = (pl.ds(half + row, 1), pl.ds(column, cells))
            keep_ref[at] = jnp.where(mine == side, lists[slot : slot + 1], keep_ref[at])
            send_ref[at] = jnp.where(mine == side, send_ref[at], lists[slot : slot + 1])
    mask = mask_ref[...].astype(F32).T
    for piece in range(pieces):
        for copy in copies(piece):
            copy.wait()
        first = piece * span
        for start in range(first, first + span, TILE):
            tile = start // TILE
            column = jnp.broadcast_to(mask[:, tile : tile + 1], (cells, TILE)).astype(BF16)
            masked_ref[:, start : start + TILE] = counts_ref[:, start : start + TILE] * column
        at = slice(first, first + span)
        term = jnp.dot(masked_ref[:, at], weight_ref[at, :], preferred_element_type=F32)
        total_ref[...] = term if piece == 0 else total_ref[...] + term
    send_ref[:half, :] = LIFT * total_ref[pl.ds((1 - mine) * half, half), :]
    keep_ref[:half, :] = LIFT * total_ref[pl.ds(mine * half, half), :]


def partial_hidden(carried, counts, mask, neighbours, peak_weight):
    cells, peaks = counts.shape
    width = peak_weight.shape[1]
    pieces = 4
    whole = pl.BlockSpec(memory_space=pltpu.VMEM)
    main = pl.BlockSpec(memory_space=pltpu.HBM)
    rows = cells // 2 + (EXTRA if carried else 0)
    return pl.pallas_call(
        functools.partial(partial_kernel, carried, pieces),
        out_shape=[pltpu.VMEM((rows, width), F32)] * 2 + [pltpu.VMEM((cells, peaks), BF16)],
        in_specs=[main] * 4,
        out_specs=[whole] * 3,
        scratch_shapes=[
            pltpu.VMEM((cells, peaks), BF16),
            pltpu.VMEM(mask.shape, jnp.int32),
            pltpu.VMEM(neighbours.shape, jnp.int32),
            pltpu.VMEM((peaks, width), BF16),
            pltpu.VMEM((cells, width), F32),
            pltpu.SemaphoreType.DMA((pieces,)),
            pltpu.SemaphoreType.DMA((pieces,)),
            pltpu.SemaphoreType.DMA((2,)),
        ],
        compiler_params=pltpu.CompilerParams(
            vmem_limit_bytes=4 * MIB + 2 * (2 * cells * peaks + peaks * width) + 20 * cells * width
        ),
        cost_estimate=pl.CostEstimate(
            flops=2 * cells * peaks * width,
            bytes_accessed=4 * cells * peaks + 2 * peaks * width + 8 * rows * width,
            transcendentals=0,
        ),
    )(*(pltpu.with_memory_space_constraint(x, pltpu.HBM) for x in (counts, mask, neighbours, peak_weight)))


def turn_kernel(masked_ref, turned_ref):
    for start in range(0, masked_ref.shape[1], TILE):
        turned_ref[start : start + TILE, :] = masked_ref[:, start : start + TILE].T


def turn(masked):
    cells, peaks = masked.shape
    whole = pl.BlockSpec(memory_space=pltpu.VMEM)
    return pl.pallas_call(
        turn_kernel,
        out_shape=pltpu.VMEM((peaks, cells), BF16),
        in_specs=[whole],
        out_specs=whole,
        compiler_params=pltpu.CompilerParams(vmem_limit_bytes=4 * MIB + 6 * cells * peaks),
        cost_estimate=pl.CostEstimate(
            flops=cells * peaks, bytes_accessed=4 * cells * peaks, transcendentals=0
        ),
    )(pltpu.with_memory_space_constraint(masked, pltpu.VMEM))


def tower_kernel(
    carried, length_of, pieces, own_ref, other_ref, lists_ref, turned_ref, gain_ref, w_in_ref, w_out_ref,
    peak_grad_hbm, gain_grad_ref, in_grad_hbm, out_grad_hbm,
    hidden_ref, peak_grad_ref, in_grad_ref, out_grad_ref, peak_sem, side_sem,
):
    cells = hidden_ref.shape[0]
    half = cells // 2
    mine = own_half()
    hidden_ref[pl.ds(mine * half, half), :] = own_ref[:half, :] * (1.0 / LIFT)
    hidden_ref[pl.ds((1 - mine) * half, half), :] = other_ref[:half, :] * (1.0 / LIFT)

    def list_row(slot):
        if not carried:
            return lists_ref[slot : slot + 1, :].astype(F32)
        side, row, column = list_places(length_of, cells, own_ref.shape[1])[slot]
        at = (pl.ds(half + row, 1), pl.ds(column, cells))
        return jnp.where(mine == side, own_ref[at], other_ref[at])

    gain = gain_ref[...]
    w_in, w_out = w_in_ref[...], w_out_ref[...]

    hidden = hidden_ref[...]
    scale = lax.rsqrt(jnp.mean(hidden * hidden, axis=1, keepdims=True) + eps_norm)
    normed = hidden * scale
    rounded = (normed * gain).astype(BF16)
    preact = jnp.dot(rounded, w_in, preferred_element_type=F32)
    square = preact * preact
    tangent = jnp.tanh(gelu_coef * preact * (1.0 + cubic_coef * square))
    activ = (0.5 * preact * (1.0 + tangent)).astype(BF16)
    slope = 0.5 * (1.0 + tangent) + 0.5 * preact * (1.0 - tangent * tangent) * gelu_coef * (
        1.0 + 3.0 * cubic_coef * square
    )
    project = jnp.dot(activ, w_out, preferred_element_type=F32)
    length = lax.rsqrt(jnp.sum(project * project, axis=1, keepdims=True) + eps_norm)
    unit = project * length
    codes = unit.astype(BF16)

    scores = dot(codes, codes, 1, 1) / sharpness_divisor
    targets = lax.broadcasted_iota(jnp.int32, (cells, cells), 0)
    sources = lax.broadcasted_iota(jnp.int32, (cells, cells), 1)
    expo = jnp.where(targets == sources, 0.0, jnp.exp(scores))
    prob = expo * (1.0 / jnp.sum(expo, axis=0, keepdims=True))
    places = targets.astype(F32)
    tallies = jnp.zeros((cells, cells), F32)
    for slot in range(length_of):
        tallies = tallies + (list_row(slot) == places).astype(F32)
    coupling = (prob - tallies / length_of).astype(BF16)
    dcodes = (dot(coupling, codes, 0, 0) + dot(coupling, codes, 1, 0)) / sharpness_divisor

    dproj = (length * (dcodes - unit * jnp.sum(unit * dcodes, axis=1, keepdims=True))).astype(BF16)
    dpre = (dot(dproj, w_out, 1, 1) * slope).astype(BF16)
    dround = dot(dpre, w_in, 1, 1)
    gain_grad_ref[...] = jnp.sum(dround * normed, axis=0, keepdims=True)
    dnorm = dround * gain
    dhidden = (scale * (dnorm - normed * jnp.mean(dnorm * normed, axis=1, keepdims=True))).astype(BF16)

    span = turned_ref.shape[0] // pieces

    def peak_copy(piece):
        at = pl.ds(piece * span, span)
        return pltpu.make_async_copy(peak_grad_ref.at[at, :], peak_grad_hbm.at[at, :], peak_sem.at[piece])

    for piece in range(pieces):
        at = pl.ds(piece * span, span)
        peak_grad_ref[at, :] = jnp.dot(turned_ref[at, :], dhidden, preferred_element_type=F32)
        peak_copy(piece).start()
    in_copy = pltpu.make_async_copy(in_grad_ref, in_grad_hbm, side_sem.at[0])
    out_copy = pltpu.make_async_copy(out_grad_ref, out_grad_hbm, side_sem.at[1])
    in_grad_ref[...] = dot(rounded, dpre, 0, 0)
    in_copy.start()
    out_grad_ref[...] = dot(activ, dproj, 0, 0)
    out_copy.start()
    for piece in range(pieces):
        peak_copy(piece).wait()
    in_copy.wait()
    out_copy.wait()


def tower(carried, length_of, own, other, lists, turned, gain, w_in, w_out):
    peaks, cells = turned.shape
    width, hid = w_in.shape
    codes = w_out.shape[1]
    pieces = 8
    whole = pl.BlockSpec(memory_space=pltpu.VMEM)
    main = pl.BlockSpec(memory_space=pltpu.HBM)
    return pl.pallas_call(
        functools.partial(tower_kernel, carried, length_of, pieces),
        out_shape=[
            jax.ShapeDtypeStruct((peaks, width), F32),
            jax.ShapeDtypeStruct((1, width), F32),
            jax.ShapeDtypeStruct((width, hid), F32),
            jax.ShapeDtypeStruct((hid, codes), F32),
        ],
        in_specs=[whole] * 7,
        out_specs=[main, whole, main, main],
        scratch_shapes=[
            pltpu.VMEM((cells, width), F32),
            pltpu.VMEM((peaks, width), F32),
            pltpu.VMEM((width, hid), F32),
            pltpu.VMEM((hid, codes), F32),
            pltpu.SemaphoreType.DMA((pieces,)),
            pltpu.SemaphoreType.DMA((2,)),
        ],
        compiler_params=pltpu.CompilerParams(
            vmem_limit_bytes=min(
                56 * MIB,
                4 * (MIB + peaks * width + width * hid + hid * codes) + cells * (64 * width + 20 * cells),
            )
        ),
        cost_estimate=pl.CostEstimate(
            flops=2 * cells * width * (peaks + 3 * hid + 3 * codes),
            bytes_accessed=2 * peaks * cells + 4 * peaks * width + 6 * width * hid + 6 * hid * codes,
            transcendentals=cells * (hid + cells),
        ),
    )(own, other, lists, turned, gain, w_in, w_out)


def flips(n_grp, n_peak):
    grp_bits = [bit * n_peak for bit in (2, 4, 8, 16, 32, 64) if bit < n_grp]
    peak_bits = [bit for bit in (1, 2, 4, 8, 16, 32, 64) if bit < n_peak]
    order = grp_bits + peak_bits
    if len(order) == 4:
        order = [order[0], order[2], order[1], order[3]]
    swapped = list(order)
    for at in range(0, len(order) - 1, 2):
        swapped[at], swapped[at + 1] = order[at + 1], order[at]
    return list(zip(order, swapped, strict=True))


def body(n_grp, n_peak, counts, tile_mask, neighbours, peak_weight, gain, w_in, w_out):
    cells = counts.shape[0]
    length_of = neighbours.shape[1]
    carried = cells <= peak_weight.shape[1] and 1 + max(
        row for _, row, _ in list_places(length_of, cells, peak_weight.shape[1])
    ) <= EXTRA
    devices = n_grp * n_peak

    def exchange(values, bits):
        pairs = [(i, i ^ bits[i.bit_count() % 2]) for i in range(devices)]
        return lax.ppermute(values, ALL, pairs)

    def add(left, right):
        return lax.optimization_barrier((left.astype(F32) + right.astype(F32)).astype(LINK))

    mask = tile_mask.T
    send, held, masked = partial_hidden(carried, counts, mask, neighbours, peak_weight)
    held = add(held, exchange(send, (n_peak, n_peak)))
    turned = turn(masked)
    steps = flips(n_grp, n_peak)
    for at, bits in enumerate(steps):
        held = add(held, exchange(held, tuple(bit ^ n_peak for bit in bits)))
        if at == len(steps) // 2:
            held, turned = lax.optimization_barrier((held, turned))
    other = exchange(held, (n_peak, n_peak)).astype(F32)
    held = held.astype(F32)
    if carried:
        lists = neighbours
    else:
        lists = lax.all_gather(neighbours, ALL, axis=0, tiled=True).T
    peak_grad, gain_grad, in_grad, out_grad = tower(
        carried, length_of, held, other, lists, turned, gain.reshape(1, -1), w_in, w_out
    )
    return (peak_grad, gain_grad.reshape(-1), in_grad, out_grad)


def solution(mesh):
    placed = (
        P(None, ALL),
        P(None, ALL),
        P(ALL, None),
        P(ALL, None),
        P(),
        P(),
        P(),
    )
    return jax.shard_map(
        functools.partial(body, mesh.shape["grp"], mesh.shape["peak"]),
        mesh=mesh,
        in_specs=placed,
        out_specs=(P(ALL, None), P(), P(), P()),
        check_vma=False,
    )
```

```python
import functools

import jax
import jax.numpy as jnp
from jax import lax
from jax.experimental import pallas as pl
from jax.experimental.pallas import tpu as pltpu
from jax.sharding import PartitionSpec as P

TILE = 128
EXTRA = 8
ALL = ("grp", "peak")
MIB = 1024 * 1024
F32 = jnp.float32
BF16 = jnp.bfloat16
LINK = jnp.float16
LIFT = 2.0

sharpness_divisor = 0.2
eps_norm = 1e-06
gelu_coef = 0.7978845608
cubic_coef = 0.044715


def dot(left, right, left_dim, right_dim):
    return lax.dot_general(
        left, right, (((left_dim,), (right_dim,)), ((), ())), preferred_element_type=F32
    )


def place():
    return lax.axis_index("grp") * lax.axis_size("peak") + lax.axis_index("peak")


def own_half():
    position = place()
    ones = position
    for bit in range(1, (lax.axis_size("grp") * lax.axis_size("peak")).bit_length()):
        ones = ones + lax.shift_right_logical(position, bit)
    return lax.rem(ones, 2)


def list_places(length, cells, width):
    half = -(-length // 2)
    across = width // cells
    return [(slot // half, slot % half // across, slot % half % across * cells) for slot in range(length)]


def partial_kernel(
    carried, pieces, counts_hbm, mask_hbm, lists_hbm, weight_hbm, send_ref, keep_ref, masked_ref,
    counts_ref, mask_ref, lists_ref, weight_ref, total_ref, counts_sem, weight_sem, side_sem,
):
    cells, peaks = counts_ref.shape
    half = cells // 2
    span = peaks // pieces

    def copies(piece):
        at = pl.ds(piece * span, span)
        return (
            pltpu.make_async_copy(counts_hbm.at[:, at], counts_ref.at[:, at], counts_sem.at[piece]),
            pltpu.make_async_copy(weight_hbm.at[at, :], weight_ref.at[at, :], weight_sem.at[piece]),
        )

    sides = (
        pltpu.make_async_copy(mask_hbm, mask_ref, side_sem.at[0]),
        pltpu.make_async_copy(lists_hbm, lists_ref, side_sem.at[1]),
    )
    for copy in sides:
        copy.start()
    for piece in range(pieces):
        for copy in copies(piece):
            copy.start()
    for copy in sides:
        copy.wait()
    mine = own_half()
    if carried:
        own, length = lists_ref.shape
        columns = lax.broadcasted_iota(jnp.int32, (own, cells), 1)
        rows = lax.broadcasted_iota(jnp.int32, (own, cells), 0)
        lists = dot(lists_ref[...].astype(F32), (columns == rows + place() * own).astype(F32), 0, 0)
        send_ref[half:, :] = jnp.zeros((EXTRA, send_ref.shape[1]), F32)
        keep_ref[half:, :] = jnp.zeros((EXTRA, keep_ref.shape[1]), F32)
        for slot, (side, row, column) in enumerate(list_places(length, cells, keep_ref.shape[1])):
            at = (pl.ds(half + row, 1), pl.ds(column, cells))
            keep_ref[at] = jnp.where(mine == side, lists[slot : slot + 1], keep_ref[at])
            send_ref[at] = jnp.where(mine == side, send_ref[at], lists[slot : slot + 1])
    mask = mask_ref[...].astype(F32).T
    for piece in range(pieces):
        for copy in copies(piece):
            copy.wait()
        first = piece * span
        for start in range(first, first + span, TILE):
            tile = start // TILE
            column = jnp.broadcast_to(mask[:, tile : tile + 1], (cells, TILE)).astype(BF16)
            masked_ref[:, start : start + TILE] = counts_ref[:, start : start + TILE] * column
        at = slice(first, first + span)
        term = jnp.dot(masked_ref[:, at], weight_ref[at, :], preferred_element_type=F32)
        total_ref[...] = term if piece == 0 else total_ref[...] + term
    send_ref[:half, :] = LIFT * total_ref[pl.ds((1 - mine) * half, half), :]
    keep_ref[:half, :] = LIFT * total_ref[pl.ds(mine * half, half), :]


def partial_hidden(carried, counts, mask, neighbours, peak_weight):
    cells, peaks = counts.shape
    width = peak_weight.shape[1]
    pieces = 4
    whole = pl.BlockSpec(memory_space=pltpu.VMEM)
    main = pl.BlockSpec(memory_space=pltpu.HBM)
    rows = cells // 2 + (EXTRA if carried else 0)
    return pl.pallas_call(
        functools.partial(partial_kernel, carried, pieces),
        out_shape=[pltpu.VMEM((rows, width), F32)] * 2 + [pltpu.VMEM((cells, peaks), BF16)],
        in_specs=[main] * 4,
        out_specs=[whole] * 3,
        scratch_shapes=[
            pltpu.VMEM((cells, peaks), BF16),
            pltpu.VMEM(mask.shape, jnp.int32),
            pltpu.VMEM(neighbours.shape, jnp.int32),
            pltpu.VMEM((peaks, width), BF16),
            pltpu.VMEM((cells, width), F32),
            pltpu.SemaphoreType.DMA((pieces,)),
            pltpu.SemaphoreType.DMA((pieces,)),
            pltpu.SemaphoreType.DMA((2,)),
        ],
        compiler_params=pltpu.CompilerParams(
            vmem_limit_bytes=4 * MIB + 2 * (2 * cells * peaks + peaks * width) + 20 * cells * width
        ),
        cost_estimate=pl.CostEstimate(
            flops=2 * cells * peaks * width,
            bytes_accessed=4 * cells * peaks + 2 * peaks * width + 8 * rows * width,
            transcendentals=0,
        ),
    )(*(pltpu.with_memory_space_constraint(x, pltpu.HBM) for x in (counts, mask, neighbours, peak_weight)))


def turn_kernel(masked_ref, turned_ref):
    for start in range(0, masked_ref.shape[1], TILE):
        turned_ref[start : start + TILE, :] = masked_ref[:, start : start + TILE].T


def turn(masked):
    cells, peaks = masked.shape
    whole = pl.BlockSpec(memory_space=pltpu.VMEM)
    return pl.pallas_call(
        turn_kernel,
        out_shape=pltpu.VMEM((peaks, cells), BF16),
        in_specs=[whole],
        out_specs=whole,
        compiler_params=pltpu.CompilerParams(vmem_limit_bytes=4 * MIB + 6 * cells * peaks),
        cost_estimate=pl.CostEstimate(
            flops=cells * peaks, bytes_accessed=4 * cells * peaks, transcendentals=0
        ),
    )(pltpu.with_memory_space_constraint(masked, pltpu.VMEM))


def tower_kernel(
    carried, length_of, pieces, own_ref, other_ref, lists_ref, turned_ref, gain_ref, w_in_ref, w_out_ref,
    peak_grad_hbm, gain_grad_hbm, in_grad_hbm, out_grad_hbm,
    hidden_ref, peak_grad_ref, gain_grad_ref, in_grad_ref, out_grad_ref, peak_sem, side_sem,
):
    cells = hidden_ref.shape[0]
    half = cells // 2
    gain_copy = pltpu.make_async_copy(gain_grad_ref, gain_grad_hbm, side_sem.at[0])
    in_copy = pltpu.make_async_copy(in_grad_ref, in_grad_hbm, side_sem.at[1])
    out_copy = pltpu.make_async_copy(out_grad_ref, out_grad_hbm, side_sem.at[2])
    mine = own_half()
    hidden_ref[pl.ds(mine * half, half), :] = own_ref[:half, :] * (1.0 / LIFT)
    hidden_ref[pl.ds((1 - mine) * half, half), :] = other_ref[:half, :] * (1.0 / LIFT)

    def list_row(slot):
        if not carried:
            return lists_ref[slot : slot + 1, :].astype(F32)
        side, row, column = list_places(length_of, cells, own_ref.shape[1])[slot]
        at = (pl.ds(half + row, 1), pl.ds(column, cells))
        return jnp.where(mine == side, own_ref[at], other_ref[at])

    gain = gain_ref[...]
    w_in, w_out = w_in_ref[...], w_out_ref[...]

    hidden = hidden_ref[...]
    scale = lax.rsqrt(jnp.mean(hidden * hidden, axis=1, keepdims=True) + eps_norm)
    normed = hidden * scale
    rounded = (normed * gain).astype(BF16)
    preact = jnp.dot(rounded, w_in, preferred_element_type=F32)
    square = preact * preact
    tangent = jnp.tanh(gelu_coef * preact * (1.0 + cubic_coef * square))
    activ = (0.5 * preact * (1.0 + tangent)).astype(BF16)
    slope = 0.5 * (1.0 + tangent) + 0.5 * preact * (1.0 - tangent * tangent) * gelu_coef * (
        1.0 + 3.0 * cubic_coef * square
    )
    project = jnp.dot(activ, w_out, preferred_element_type=F32)
    length = lax.rsqrt(jnp.sum(project * project, axis=1, keepdims=True) + eps_norm)
    unit = project * length
    codes = unit.astype(BF16)

    scores = dot(codes, codes, 1, 1) / sharpness_divisor
    targets = lax.broadcasted_iota(jnp.int32, (cells, cells), 0)
    sources = lax.broadcasted_iota(jnp.int32, (cells, cells), 1)
    expo = jnp.where(targets == sources, 0.0, jnp.exp(scores))
    prob = expo * (1.0 / jnp.sum(expo, axis=0, keepdims=True))
    places = targets.astype(F32)
    tallies = jnp.zeros((cells, cells), F32)
    for slot in range(length_of):
        tallies = tallies + (list_row(slot) == places).astype(F32)
    coupling = (prob - tallies / length_of).astype(BF16)
    dcodes = (dot(coupling, codes, 0, 0) + dot(coupling, codes, 1, 0)) / sharpness_divisor

    dproj = (length * (dcodes - unit * jnp.sum(unit * dcodes, axis=1, keepdims=True))).astype(BF16)
    dpre = (dot(dproj, w_out, 1, 1) * slope).astype(BF16)
    out_grad_ref[...] = dot(activ, dproj, 0, 0)
    out_copy.start()
    dround = dot(dpre, w_in, 1, 1)
    in_grad_ref[...] = dot(rounded, dpre, 0, 0)
    in_copy.start()
    gain_grad_ref[...] = jnp.sum(dround * normed, axis=0, keepdims=True)
    gain_copy.start()
    dnorm = dround * gain
    dhidden = (scale * (dnorm - normed * jnp.mean(dnorm * normed, axis=1, keepdims=True))).astype(BF16)

    span = turned_ref.shape[0] // pieces

    def peak_copy(piece):
        at = pl.ds(piece * span, span)
        return pltpu.make_async_copy(peak_grad_ref.at[at, :], peak_grad_hbm.at[at, :], peak_sem.at[piece])

    @pl.loop(0, 2)
    def _(part):
        for inner in range(pieces // 2):
            piece = part * (pieces // 2) + inner
            at = pl.ds(pl.multiple_of(piece * span, span), span)
            peak_grad_ref[at, :] = jnp.dot(turned_ref[at, :], dhidden, preferred_element_type=F32)
            peak_copy(piece).start()

    for piece in range(pieces):
        peak_copy(piece).wait()
    gain_copy.wait()
    in_copy.wait()
    out_copy.wait()


def tower(carried, length_of, own, other, lists, turned, gain, w_in, w_out):
    peaks, cells = turned.shape
    width, hid = w_in.shape
    codes = w_out.shape[1]
    pieces = 4
    whole = pl.BlockSpec(memory_space=pltpu.VMEM)
    main = pl.BlockSpec(memory_space=pltpu.HBM)
    return pl.pallas_call(
        functools.partial(tower_kernel, carried, length_of, pieces),
        out_shape=[
            jax.ShapeDtypeStruct((peaks, width), F32),
            jax.ShapeDtypeStruct((1, width), F32),
            jax.ShapeDtypeStruct((width, hid), F32),
            jax.ShapeDtypeStruct((hid, codes), F32),
        ],
        in_specs=[whole] * 7,
        out_specs=[main] * 4,
        scratch_shapes=[
            pltpu.VMEM((cells, width), F32),
            pltpu.VMEM((peaks, width), F32),
            pltpu.VMEM((1, width), F32),
            pltpu.VMEM((width, hid), F32),
            pltpu.VMEM((hid, codes), F32),
            pltpu.SemaphoreType.DMA((pieces,)),
            pltpu.SemaphoreType.DMA((3,)),
        ],
        compiler_params=pltpu.CompilerParams(
            vmem_limit_bytes=min(
                56 * MIB,
                4 * (MIB + peaks * width + width * hid + hid * codes) + cells * (64 * width + 20 * cells),
            )
        ),
        cost_estimate=pl.CostEstimate(
            flops=2 * cells * width * (peaks + 3 * hid + 3 * codes),
            bytes_accessed=2 * peaks * cells + 4 * peaks * width + 6 * width * hid + 6 * hid * codes,
            transcendentals=cells * (hid + cells),
        ),
    )(own, other, lists, turned, gain, w_in, w_out)


def flips(n_grp, n_peak):
    grp_bits = [bit * n_peak for bit in (2, 4, 8, 16, 32, 64) if bit < n_grp]
    peak_bits = [bit for bit in (1, 2, 4, 8, 16, 32, 64) if bit < n_peak]
    order = grp_bits + peak_bits
    if len(order) == 4:
        order = [order[0], order[2], order[1], order[3]]
    swapped = list(order)
    for at in range(0, len(order) - 1, 2):
        swapped[at], swapped[at + 1] = order[at + 1], order[at]
    return list(zip(order, swapped, strict=True))


def body(n_grp, n_peak, counts, tile_mask, neighbours, peak_weight, gain, w_in, w_out):
    cells = counts.shape[0]
    length_of = neighbours.shape[1]
    carried = cells <= peak_weight.shape[1] and 1 + max(
        row for _, row, _ in list_places(length_of, cells, peak_weight.shape[1])
    ) <= EXTRA
    devices = n_grp * n_peak

    def exchange(values, bits):
        pairs = [(i, i ^ bits[i.bit_count() % 2]) for i in range(devices)]
        return lax.ppermute(values, ALL, pairs)

    def add(left, right):
        return lax.optimization_barrier((left.astype(F32) + right.astype(F32)).astype(LINK))

    mask = tile_mask.T
    send, held, masked = partial_hidden(carried, counts, mask, neighbours, peak_weight)
    held = add(held, exchange(send, (n_peak, n_peak)))
    turned = turn(masked)
    steps = flips(n_grp, n_peak)
    for at, bits in enumerate(steps):
        held = add(held, exchange(held, tuple(bit ^ n_peak for bit in bits)))
        if at == len(steps) // 2:
            held, turned = lax.optimization_barrier((held, turned))
    other = exchange(held, (n_peak, n_peak)).astype(F32)
    held = held.astype(F32)
    if carried:
        lists = neighbours
    else:
        lists = lax.all_gather(neighbours, ALL, axis=0, tiled=True).T
    peak_grad, gain_grad, in_grad, out_grad = tower(
        carried, length_of, held, other, lists, turned, gain.reshape(1, -1), w_in, w_out
    )
    return (peak_grad, gain_grad.reshape(-1), in_grad, out_grad)


def solution(mesh):
    placed = (
        P(None, ALL),
        P(None, ALL),
        P(ALL, None),
        P(ALL, None),
        P(),
        P(),
        P(),
    )
    return jax.shard_map(
        functools.partial(body, mesh.shape["grp"], mesh.shape["peak"]),
        mesh=mesh,
        in_specs=placed,
        out_specs=(P(ALL, None), P(), P(), P()),
        check_vma=False,
    )
```

```python
import functools

import jax
import jax.numpy as jnp
from jax import lax
from jax.experimental import pallas as pl
from jax.experimental.pallas import tpu as pltpu
from jax.sharding import PartitionSpec as P

TILE = 128
SLOTS = 8
ALL = ("grp", "peak")
MIB = 1024 * 1024
F32 = jnp.float32
BF16 = jnp.bfloat16
LINK = jnp.float16
LIFT = 2.0

sharpness_divisor = 0.2
eps_norm = 1e-06
gelu_coef = 0.7978845608
cubic_coef = 0.044715


def dot(left, right, left_dim, right_dim):
    return lax.dot_general(
        left, right, (((left_dim,), (right_dim,)), ((), ())), preferred_element_type=F32
    )


def place():
    return lax.axis_index("grp") * lax.axis_size("peak") + lax.axis_index("peak")


def own_half():
    position = place()
    ones = position
    for bit in range(1, (lax.axis_size("grp") * lax.axis_size("peak")).bit_length()):
        ones = ones + lax.shift_right_logical(position, bit)
    return lax.rem(ones, 2)


def tiles_of(rows, columns):
    return rows // 8 * (columns // TILE)


def to_tiles(values):
    rows, columns = values.shape
    return [values[:, start : start + TILE].reshape(rows // 8, 8, TILE) for start in range(0, columns, TILE)]


def partial_kernel(
    carried, pieces, counts_hbm, mask_hbm, lists_hbm, weight_hbm, send_ref, keep_ref, masked_ref,
    counts_ref, mask_ref, lists_ref, weight_ref, total_ref, counts_sem, weight_sem, side_sem,
):
    cells, peaks = counts_ref.shape
    half = cells // 2
    span = peaks // pieces

    def copies(piece):
        at = pl.ds(piece * span, span)
        return (
            pltpu.make_async_copy(counts_hbm.at[:, at], counts_ref.at[:, at], counts_sem.at[piece]),
            pltpu.make_async_copy(weight_hbm.at[at, :], weight_ref.at[at, :], weight_sem.at[piece]),
        )

    sides = (
        pltpu.make_async_copy(mask_hbm, mask_ref, side_sem.at[0]),
        pltpu.make_async_copy(lists_hbm, lists_ref, side_sem.at[1]),
    )
    for copy in sides:
        copy.start()
    for piece in range(pieces):
        for copy in copies(piece):
            copy.start()
    for copy in sides:
        copy.wait()
    mine = own_half()
    if carried:
        own, length = lists_ref.shape
        columns = lax.broadcasted_iota(jnp.int32, (own, cells), 1)
        rows = lax.broadcasted_iota(jnp.int32, (own, cells), 0)
        lists = dot(lists_ref[...].astype(F32), (columns == rows + place() * own).astype(F32), 0, 0)
        lists = jnp.concatenate([lists, jnp.zeros((2 * SLOTS - length, cells), F32)], axis=0)
        low, high = lists[:SLOTS], lists[SLOTS:]
        first = tiles_of(half, total_ref.shape[1])
        for at, (low_tile, high_tile) in enumerate(zip(to_tiles(low), to_tiles(high), strict=True), first):
            keep_ref[at : at + 1] = jnp.where(mine == 0, low_tile, high_tile)
            send_ref[at : at + 1] = jnp.where(mine == 0, high_tile, low_tile)
    mask = mask_ref[...].astype(F32).T
    for piece in range(pieces):
        for copy in copies(piece):
            copy.wait()
        first = piece * span
        for start in range(first, first + span, TILE):
            tile = start // TILE
            column = jnp.broadcast_to(mask[:, tile : tile + 1], (cells, TILE)).astype(BF16)
            masked_ref[:, start : start + TILE] = counts_ref[:, start : start + TILE] * column
        at = slice(first, first + span)
        term = jnp.dot(masked_ref[:, at], weight_ref[at, :], preferred_element_type=F32)
        total_ref[...] = term if piece == 0 else total_ref[...] + term
    for ref, side in ((send_ref, 1 - mine), (keep_ref, mine)):
        for at, tiles in enumerate(to_tiles(LIFT * total_ref[pl.ds(side * half, half), :])):
            ref[at * (half // 8) : (at + 1) * (half // 8)] = tiles


def partial_hidden(carried, counts, mask, neighbours, peak_weight):
    cells, peaks = counts.shape
    width = peak_weight.shape[1]
    pieces = 2
    whole = pl.BlockSpec(memory_space=pltpu.VMEM)
    main = pl.BlockSpec(memory_space=pltpu.HBM)
    tiles = tiles_of(cells // 2, width) + (tiles_of(SLOTS, cells) if carried else 0)
    return pl.pallas_call(
        functools.partial(partial_kernel, carried, pieces),
        out_shape=[pltpu.VMEM((tiles, 8, TILE), F32)] * 2 + [pltpu.VMEM((cells, peaks), BF16)],
        in_specs=[main] * 4,
        out_specs=[whole] * 3,
        scratch_shapes=[
            pltpu.VMEM((cells, peaks), BF16),
            pltpu.VMEM(mask.shape, jnp.int32),
            pltpu.VMEM(neighbours.shape, jnp.int32),
            pltpu.VMEM((peaks, width), BF16),
            pltpu.VMEM((cells, width), F32),
            pltpu.SemaphoreType.DMA((pieces,)),
            pltpu.SemaphoreType.DMA((pieces,)),
            pltpu.SemaphoreType.DMA((2,)),
        ],
        compiler_params=pltpu.CompilerParams(
            vmem_limit_bytes=4 * MIB + 2 * (2 * cells * peaks + peaks * width) + 20 * cells * width
        ),
        cost_estimate=pl.CostEstimate(
            flops=2 * cells * peaks * width,
            bytes_accessed=4 * cells * peaks + 2 * peaks * width + 64 * tiles * TILE,
            transcendentals=0,
        ),
    )(*(pltpu.with_memory_space_constraint(x, pltpu.HBM) for x in (counts, mask, neighbours, peak_weight)))


def turn_kernel(masked_ref, turned_ref):
    for start in range(0, masked_ref.shape[1], TILE):
        turned_ref[start : start + TILE, :] = masked_ref[:, start : start + TILE].T


def turn(masked):
    cells, peaks = masked.shape
    whole = pl.BlockSpec(memory_space=pltpu.VMEM)
    return pl.pallas_call(
        turn_kernel,
        out_shape=pltpu.VMEM((peaks, cells), BF16),
        in_specs=[whole],
        out_specs=whole,
        compiler_params=pltpu.CompilerParams(vmem_limit_bytes=4 * MIB + 6 * cells * peaks),
        cost_estimate=pl.CostEstimate(
            flops=cells * peaks, bytes_accessed=4 * cells * peaks, transcendentals=0
        ),
    )(pltpu.with_memory_space_constraint(masked, pltpu.VMEM))


def tower_kernel(
    carried, length_of, pieces, own_ref, other_ref, lists_ref, turned_ref, gain_ref, w_in_ref, w_out_ref,
    peak_grad_hbm, gain_grad_hbm, in_grad_hbm, out_grad_hbm,
    hidden_ref, peak_grad_ref, gain_grad_ref, in_grad_ref, out_grad_ref, peak_sem, side_sem,
):
    cells = hidden_ref.shape[0]
    half = cells // 2
    gain_copy = pltpu.make_async_copy(gain_grad_ref, gain_grad_hbm, side_sem.at[0])
    in_copy = pltpu.make_async_copy(in_grad_ref, in_grad_hbm, side_sem.at[1])
    out_copy = pltpu.make_async_copy(out_grad_ref, out_grad_hbm, side_sem.at[2])
    mine = own_half()
    for ref, side in ((own_ref, mine), (other_ref, 1 - mine)):
        for at in range(hidden_ref.shape[1] // TILE):
            tiles = ref[at * (half // 8) : (at + 1) * (half // 8)]
            hidden_ref[pl.ds(side * half, half), at * TILE : (at + 1) * TILE] = tiles.reshape(half, TILE) * (1.0 / LIFT)
    if carried:
        first = tiles_of(half, hidden_ref.shape[1])
        pairs = [(own_ref[at], other_ref[at]) for at in range(first, own_ref.shape[0])]
        low = [jnp.where(mine == 0, own, other) for own, other in pairs]
        high = [jnp.where(mine == 0, other, own) for own, other in pairs]
        lists = jnp.concatenate([jnp.concatenate(low, axis=1), jnp.concatenate(high, axis=1)], axis=0)
    else:
        lists = lists_ref[...].astype(F32)
    gain = gain_ref[...]
    w_in, w_out = w_in_ref[...], w_out_ref[...]

    hidden = hidden_ref[...]
    scale = lax.rsqrt(jnp.mean(hidden * hidden, axis=1, keepdims=True) + eps_norm)
    normed = hidden * scale
    rounded = (normed * gain).astype(BF16)
    preact = jnp.dot(rounded, w_in, preferred_element_type=F32)
    square = preact * preact
    tangent = jnp.tanh(gelu_coef * preact * (1.0 + cubic_coef * square))
    activ = (0.5 * preact * (1.0 + tangent)).astype(BF16)
    slope = 0.5 * (1.0 + tangent) + 0.5 * preact * (1.0 - tangent * tangent) * gelu_coef * (
        1.0 + 3.0 * cubic_coef * square
    )
    project = jnp.dot(activ, w_out, preferred_element_type=F32)
    length = lax.rsqrt(jnp.sum(project * project, axis=1, keepdims=True) + eps_norm)
    unit = project * length
    codes = unit.astype(BF16)

    scores = dot(codes, codes, 1, 1) / sharpness_divisor
    targets = lax.broadcasted_iota(jnp.int32, (cells, cells), 0)
    sources = lax.broadcasted_iota(jnp.int32, (cells, cells), 1)
    expo = jnp.where(targets == sources, 0.0, jnp.exp(scores))
    prob = expo * (1.0 / jnp.sum(expo, axis=0, keepdims=True))
    places = targets.astype(F32)
    tallies = jnp.zeros((cells, cells), F32)
    for slot in range(length_of):
        tallies = tallies + (lists[slot : slot + 1] == places).astype(F32)
    coupling = (prob - tallies / length_of).astype(BF16)
    dcodes = (dot(coupling, codes, 0, 0) + dot(coupling, codes, 1, 0)) / sharpness_divisor

    dproj = (length * (dcodes - unit * jnp.sum(unit * dcodes, axis=1, keepdims=True))).astype(BF16)
    dpre = (dot(dproj, w_out, 1, 1) * slope).astype(BF16)
    out_grad_ref[...] = dot(activ, dproj, 0, 0)
    out_copy.start()
    dround = dot(dpre, w_in, 1, 1)
    in_grad_ref[...] = dot(rounded, dpre, 0, 0)
    in_copy.start()
    gain_grad_ref[...] = jnp.sum(dround * normed, axis=0, keepdims=True)
    gain_copy.start()
    dnorm = dround * gain
    dhidden = (scale * (dnorm - normed * jnp.mean(dnorm * normed, axis=1, keepdims=True))).astype(BF16)

    span = turned_ref.shape[0] // pieces

    def peak_copy(piece):
        at = pl.ds(piece * span, span)
        return pltpu.make_async_copy(peak_grad_ref.at[at, :], peak_grad_hbm.at[at, :], peak_sem.at[piece])

    @pl.loop(0, 2)
    def _(part):
        for inner in range(pieces // 2):
            piece = part * (pieces // 2) + inner
            at = pl.ds(pl.multiple_of(piece * span, span), span)
            peak_grad_ref[at, :] = jnp.dot(turned_ref[at, :], dhidden, preferred_element_type=F32)
            peak_copy(piece).start()

    for piece in range(pieces):
        peak_copy(piece).wait()
    gain_copy.wait()
    in_copy.wait()
    out_copy.wait()


def tower(carried, length_of, own, other, lists, turned, gain, w_in, w_out):
    peaks, cells = turned.shape
    width, hid = w_in.shape
    codes = w_out.shape[1]
    pieces = 4
    whole = pl.BlockSpec(memory_space=pltpu.VMEM)
    main = pl.BlockSpec(memory_space=pltpu.HBM)
    return pl.pallas_call(
        functools.partial(tower_kernel, carried, length_of, pieces),
        out_shape=[
            jax.ShapeDtypeStruct((peaks, width), F32),
            jax.ShapeDtypeStruct((1, width), F32),
            jax.ShapeDtypeStruct((width, hid), F32),
            jax.ShapeDtypeStruct((hid, codes), F32),
        ],
        in_specs=[whole] * 7,
        out_specs=[main] * 4,
        scratch_shapes=[
            pltpu.VMEM((cells, width), F32),
            pltpu.VMEM((peaks, width), F32),
            pltpu.VMEM((1, width), F32),
            pltpu.VMEM((width, hid), F32),
            pltpu.VMEM((hid, codes), F32),
            pltpu.SemaphoreType.DMA((pieces,)),
            pltpu.SemaphoreType.DMA((3,)),
        ],
        compiler_params=pltpu.CompilerParams(
            vmem_limit_bytes=min(
                56 * MIB,
                4 * (MIB + peaks * width + width * hid + hid * codes) + cells * (64 * width + 20 * cells),
            )
        ),
        cost_estimate=pl.CostEstimate(
            flops=2 * cells * width * (peaks + 3 * hid + 3 * codes),
            bytes_accessed=2 * peaks * cells + 4 * peaks * width + 6 * width * hid + 6 * hid * codes,
            transcendentals=cells * (hid + cells),
        ),
    )(own, other, lists, turned, gain, w_in, w_out)


def flips(n_grp, n_peak):
    grp_bits = [bit * n_peak for bit in (2, 4, 8, 16, 32, 64) if bit < n_grp]
    peak_bits = [bit for bit in (1, 2, 4, 8, 16, 32, 64) if bit < n_peak]
    order = grp_bits + peak_bits
    if len(order) == 4:
        order = [order[3], order[0], order[2], order[1]]
    swapped = list(order)
    for at in range(0, len(order) - 1, 2):
        swapped[at], swapped[at + 1] = order[at + 1], order[at]
    return list(zip(order, swapped, strict=True))


def body(n_grp, n_peak, counts, tile_mask, neighbours, peak_weight, gain, w_in, w_out):
    cells = counts.shape[0]
    length_of = neighbours.shape[1]
    carried = cells <= 512 and length_of <= 2 * SLOTS
    devices = n_grp * n_peak

    def exchange(values, bits):
        pairs = [(i, i ^ bits[i.bit_count() % 2]) for i in range(devices)]
        return lax.ppermute(values, ALL, pairs)

    def add(left, right):
        return lax.optimization_barrier((left.astype(F32) + right.astype(F32)).astype(LINK))

    mask = tile_mask.T
    send, held, masked = partial_hidden(carried, counts, mask, neighbours, peak_weight)
    held = add(held, exchange(send, (n_peak, n_peak)))
    turned = turn(masked)
    steps = flips(n_grp, n_peak)
    for at, bits in enumerate(steps):
        held = add(held, exchange(held, tuple(bit ^ n_peak for bit in bits)))
        if at == len(steps) // 2:
            held, turned = lax.optimization_barrier((held, turned))
    other = exchange(held, (n_peak, n_peak)).astype(F32)
    held = held.astype(F32)
    if carried:
        lists = neighbours
    else:
        lists = lax.all_gather(neighbours, ALL, axis=0, tiled=True).T
    peak_grad, gain_grad, in_grad, out_grad = tower(
        carried, length_of, held, other, lists, turned, gain.reshape(1, -1), w_in, w_out
    )
    return (peak_grad, gain_grad.reshape(-1), in_grad, out_grad)


def solution(mesh):
    placed = (
        P(None, ALL),
        P(None, ALL),
        P(ALL, None),
        P(ALL, None),
        P(),
        P(),
        P(),
    )
    return jax.shard_map(
        functools.partial(body, mesh.shape["grp"], mesh.shape["peak"]),
        mesh=mesh,
        in_specs=placed,
        out_specs=(P(ALL, None), P(), P(), P()),
        check_vma=False,
    )
```

```python
import functools

import jax
import jax.numpy as jnp
from jax import lax
from jax.experimental import pallas as pl
from jax.experimental.pallas import tpu as pltpu
from jax.sharding import PartitionSpec as P

TILE = 128
SLOTS = 8
ALL = ("grp", "peak")
MIB = 1024 * 1024
F32 = jnp.float32
BF16 = jnp.bfloat16
LINK = jnp.float16
LIFT = 2.0

sharpness_divisor = 0.2
eps_norm = 1e-06
gelu_coef = 0.7978845608
cubic_coef = 0.044715


def dot(left, right, left_dim, right_dim):
    return lax.dot_general(
        left, right, (((left_dim,), (right_dim,)), ((), ())), preferred_element_type=F32
    )


def place():
    return lax.axis_index("grp") * lax.axis_size("peak") + lax.axis_index("peak")


def own_half():
    position = place()
    ones = position
    for bit in range(1, (lax.axis_size("grp") * lax.axis_size("peak")).bit_length()):
        ones = ones + lax.shift_right_logical(position, bit)
    return lax.rem(ones, 2)


def tiles_of(rows, columns):
    return rows // 8 * (columns // TILE)


def to_tiles(values):
    rows, columns = values.shape
    return [values[:, start : start + TILE].reshape(rows // 8, 8, TILE) for start in range(0, columns, TILE)]


def partial_kernel(
    carried, pieces, counts_hbm, mask_hbm, lists_hbm, weight_hbm, send_ref, keep_ref, masked_ref,
    counts_ref, mask_ref, lists_ref, weight_ref, total_ref, counts_sem, weight_sem, side_sem,
):
    cells, peaks = counts_ref.shape
    half = cells // 2
    span = peaks // pieces

    def copies(piece):
        at = pl.ds(piece * span, span)
        return (
            pltpu.make_async_copy(counts_hbm.at[:, at], counts_ref.at[:, at], counts_sem.at[piece]),
            pltpu.make_async_copy(weight_hbm.at[at, :], weight_ref.at[at, :], weight_sem.at[piece]),
        )

    sides = (
        pltpu.make_async_copy(mask_hbm, mask_ref, side_sem.at[0]),
        pltpu.make_async_copy(lists_hbm, lists_ref, side_sem.at[1]),
    )
    for copy in sides:
        copy.start()
    for piece in range(pieces):
        for copy in copies(piece):
            copy.start()
    for copy in sides:
        copy.wait()
    mine = own_half()
    if carried:
        own, length = lists_ref.shape
        columns = lax.broadcasted_iota(jnp.int32, (own, cells), 1)
        rows = lax.broadcasted_iota(jnp.int32, (own, cells), 0)
        lists = dot(lists_ref[...].astype(F32), (columns == rows + place() * own).astype(F32), 0, 0)
        lists = jnp.concatenate([lists, jnp.zeros((2 * SLOTS - length, cells), F32)], axis=0)
        low, high = lists[:SLOTS], lists[SLOTS:]
        first = tiles_of(half, total_ref.shape[1])
        for at, (low_tile, high_tile) in enumerate(zip(to_tiles(low), to_tiles(high), strict=True), first):
            keep_ref[at : at + 1] = jnp.where(mine == 0, low_tile, high_tile)
            send_ref[at : at + 1] = jnp.where(mine == 0, high_tile, low_tile)
    mask = mask_ref[...].astype(F32).T
    for piece in range(pieces):
        for copy in copies(piece):
            copy.wait()
        first = piece * span
        for start in range(first, first + span, TILE):
            tile = start // TILE
            column = jnp.broadcast_to(mask[:, tile : tile + 1], (cells, TILE)).astype(BF16)
            masked_ref[:, start : start + TILE] = counts_ref[:, start : start + TILE] * column
        at = slice(first, first + span)
        term = jnp.dot(masked_ref[:, at], weight_ref[at, :], preferred_element_type=F32)
        total_ref[...] = term if piece == 0 else total_ref[...] + term
    for ref, side in ((send_ref, 1 - mine), (keep_ref, mine)):
        for at, tiles in enumerate(to_tiles(LIFT * total_ref[pl.ds(side * half, half), :])):
            ref[at * (half // 8) : (at + 1) * (half // 8)] = tiles


def partial_hidden(carried, counts, mask, neighbours, peak_weight):
    cells, peaks = counts.shape
    width = peak_weight.shape[1]
    pieces = 2
    whole = pl.BlockSpec(memory_space=pltpu.VMEM)
    main = pl.BlockSpec(memory_space=pltpu.HBM)
    tiles = tiles_of(cells // 2, width) + (tiles_of(SLOTS, cells) if carried else 0)
    return pl.pallas_call(
        functools.partial(partial_kernel, carried, pieces),
        out_shape=[pltpu.VMEM((tiles, 8, TILE), F32)] * 2 + [pltpu.VMEM((cells, peaks), BF16)],
        in_specs=[main] * 4,
        out_specs=[whole] * 3,
        scratch_shapes=[
            pltpu.VMEM((cells, peaks), BF16),
            pltpu.VMEM(mask.shape, jnp.int32),
            pltpu.VMEM(neighbours.shape, jnp.int32),
            pltpu.VMEM((peaks, width), BF16),
            pltpu.VMEM((cells, width), F32),
            pltpu.SemaphoreType.DMA((pieces,)),
            pltpu.SemaphoreType.DMA((pieces,)),
            pltpu.SemaphoreType.DMA((2,)),
        ],
        compiler_params=pltpu.CompilerParams(
            vmem_limit_bytes=4 * MIB + 2 * (2 * cells * peaks + peaks * width) + 20 * cells * width
        ),
        cost_estimate=pl.CostEstimate(
            flops=2 * cells * peaks * width,
            bytes_accessed=4 * cells * peaks + 2 * peaks * width + 64 * tiles * TILE,
            transcendentals=0,
        ),
    )(*(pltpu.with_memory_space_constraint(x, pltpu.HBM) for x in (counts, mask, neighbours, peak_weight)))


def turn_kernel(masked_ref, turned_ref):
    for start in range(0, masked_ref.shape[1], TILE):
        turned_ref[start : start + TILE, :] = masked_ref[:, start : start + TILE].T


def turn(masked):
    cells, peaks = masked.shape
    whole = pl.BlockSpec(memory_space=pltpu.VMEM)
    return pl.pallas_call(
        turn_kernel,
        out_shape=pltpu.VMEM((peaks, cells), BF16),
        in_specs=[whole],
        out_specs=whole,
        compiler_params=pltpu.CompilerParams(vmem_limit_bytes=4 * MIB + 6 * cells * peaks),
        cost_estimate=pl.CostEstimate(
            flops=cells * peaks, bytes_accessed=4 * cells * peaks, transcendentals=0
        ),
    )(pltpu.with_memory_space_constraint(masked, pltpu.VMEM))


def tower_kernel(
    carried, length_of, pieces, own_ref, other_ref, turned_ref, gain_ref, w_in_ref, w_out_ref, *refs
):
    lists_refs, refs = ((), refs) if carried else (refs[:1], refs[1:])
    peak_grad_hbm, gain_grad_hbm, in_grad_hbm, out_grad_hbm, *refs = refs
    hidden_ref, peak_grad_ref, gain_grad_ref, in_grad_ref, out_grad_ref, peak_sem, side_sem = refs
    cells = hidden_ref.shape[0]
    half = cells // 2
    gain_copy = pltpu.make_async_copy(gain_grad_ref, gain_grad_hbm, side_sem.at[0])
    in_copy = pltpu.make_async_copy(in_grad_ref, in_grad_hbm, side_sem.at[1])
    out_copy = pltpu.make_async_copy(out_grad_ref, out_grad_hbm, side_sem.at[2])
    mine = own_half()
    for ref, side in ((own_ref, mine), (other_ref, 1 - mine)):
        for at in range(hidden_ref.shape[1] // TILE):
            tiles = ref[at * (half // 8) : (at + 1) * (half // 8)]
            hidden_ref[pl.ds(side * half, half), at * TILE : (at + 1) * TILE] = tiles.reshape(half, TILE) * (1.0 / LIFT)
    if carried:
        first = tiles_of(half, hidden_ref.shape[1])
        pairs = [(own_ref[at], other_ref[at]) for at in range(first, own_ref.shape[0])]
        low = [jnp.where(mine == 0, own, other) for own, other in pairs]
        high = [jnp.where(mine == 0, other, own) for own, other in pairs]
        lists = jnp.concatenate([jnp.concatenate(low, axis=1), jnp.concatenate(high, axis=1)], axis=0)
    else:
        lists = lists_refs[0][...].astype(F32)
    gain = gain_ref[...]
    w_in, w_out = w_in_ref[...], w_out_ref[...]

    hidden = hidden_ref[...]
    scale = lax.rsqrt(jnp.mean(hidden * hidden, axis=1, keepdims=True) + eps_norm)
    normed = hidden * scale
    rounded = (normed * gain).astype(BF16)
    preact = jnp.dot(rounded, w_in, preferred_element_type=F32)
    square = preact * preact
    tangent = jnp.tanh(gelu_coef * preact * (1.0 + cubic_coef * square))
    activ = (0.5 * preact * (1.0 + tangent)).astype(BF16)
    slope = 0.5 * (1.0 + tangent) + 0.5 * preact * (1.0 - tangent * tangent) * gelu_coef * (
        1.0 + 3.0 * cubic_coef * square
    )
    project = jnp.dot(activ, w_out, preferred_element_type=F32)
    length = lax.rsqrt(jnp.sum(project * project, axis=1, keepdims=True) + eps_norm)
    unit = project * length
    codes = unit.astype(BF16)

    scores = dot(codes, codes, 1, 1) / sharpness_divisor
    targets = lax.broadcasted_iota(jnp.int32, (cells, cells), 0)
    sources = lax.broadcasted_iota(jnp.int32, (cells, cells), 1)
    expo = jnp.where(targets == sources, 0.0, jnp.exp(scores))
    prob = expo * (1.0 / jnp.sum(expo, axis=0, keepdims=True))
    places = targets.astype(F32)
    tallies = jnp.zeros((cells, cells), F32)
    for slot in range(length_of):
        tallies = tallies + (lists[slot : slot + 1] == places).astype(F32)
    coupling = (prob - tallies / length_of).astype(BF16)
    dcodes = (dot(coupling, codes, 0, 0) + dot(coupling, codes, 1, 0)) / sharpness_divisor

    dproj = (length * (dcodes - unit * jnp.sum(unit * dcodes, axis=1, keepdims=True))).astype(BF16)
    dpre = (dot(dproj, w_out, 1, 1) * slope).astype(BF16)
    out_grad_ref[...] = dot(activ, dproj, 0, 0)
    out_copy.start()
    dround = dot(dpre, w_in, 1, 1)
    in_grad_ref[...] = dot(rounded, dpre, 0, 0)
    in_copy.start()
    gain_grad_ref[...] = jnp.sum(dround * normed, axis=0, keepdims=True)
    gain_copy.start()
    dnorm = dround * gain
    dhidden = (scale * (dnorm - normed * jnp.mean(dnorm * normed, axis=1, keepdims=True))).astype(BF16)

    span = turned_ref.shape[0] // pieces

    def peak_copy(piece):
        at = pl.ds(piece * span, span)
        return pltpu.make_async_copy(peak_grad_ref.at[at, :], peak_grad_hbm.at[at, :], peak_sem.at[piece])

    @pl.loop(0, 2)
    def _(part):
        for inner in range(pieces // 2):
            piece = part * (pieces // 2) + inner
            at = pl.ds(pl.multiple_of(piece * span, span), span)
            peak_grad_ref[at, :] = jnp.dot(turned_ref[at, :], dhidden, preferred_element_type=F32)
            peak_copy(piece).start()

    for piece in range(pieces):
        peak_copy(piece).wait()
    gain_copy.wait()
    in_copy.wait()
    out_copy.wait()


def tower(carried, length_of, own, other, turned, gain, w_in, w_out, *lists):
    peaks, cells = turned.shape
    width, hid = w_in.shape
    codes = w_out.shape[1]
    pieces = 4
    whole = pl.BlockSpec(memory_space=pltpu.VMEM)
    main = pl.BlockSpec(memory_space=pltpu.HBM)
    return pl.pallas_call(
        functools.partial(tower_kernel, carried, length_of, pieces),
        out_shape=[
            jax.ShapeDtypeStruct((peaks, width), F32),
            jax.ShapeDtypeStruct((1, width), F32),
            jax.ShapeDtypeStruct((width, hid), F32),
            jax.ShapeDtypeStruct((hid, codes), F32),
        ],
        in_specs=[whole] * (6 + len(lists)),
        out_specs=[main] * 4,
        scratch_shapes=[
            pltpu.VMEM((cells, width), F32),
            pltpu.VMEM((peaks, width), F32),
            pltpu.VMEM((1, width), F32),
            pltpu.VMEM((width, hid), F32),
            pltpu.VMEM((hid, codes), F32),
            pltpu.SemaphoreType.DMA((pieces,)),
            pltpu.SemaphoreType.DMA((3,)),
        ],
        compiler_params=pltpu.CompilerParams(
            vmem_limit_bytes=min(
                56 * MIB,
                4 * (MIB + peaks * width + width * hid + hid * codes) + cells * (64 * width + 20 * cells),
            )
        ),
        cost_estimate=pl.CostEstimate(
            flops=2 * cells * width * (peaks + 3 * hid + 3 * codes),
            bytes_accessed=2 * peaks * cells + 4 * peaks * width + 6 * width * hid + 6 * hid * codes,
            transcendentals=cells * (hid + cells),
        ),
    )(own, other, turned, gain, w_in, w_out, *lists)


def flips(n_grp, n_peak):
    grp_bits = [bit * n_peak for bit in (2, 4, 8, 16, 32, 64) if bit < n_grp]
    peak_bits = [bit for bit in (1, 2, 4, 8, 16, 32, 64) if bit < n_peak]
    order = grp_bits + peak_bits
    if len(order) == 4:
        order = [order[3], order[0], order[2], order[1]]
    swapped = list(order)
    for at in range(0, len(order) - 1, 2):
        swapped[at], swapped[at + 1] = order[at + 1], order[at]
    return list(zip(order, swapped, strict=True))


def body(n_grp, n_peak, counts, tile_mask, neighbours, peak_weight, gain, w_in, w_out):
    cells = counts.shape[0]
    length_of = neighbours.shape[1]
    carried = cells <= 512 and length_of <= 2 * SLOTS
    devices = n_grp * n_peak

    def exchange(values, bits):
        pairs = [(i, i ^ bits[i.bit_count() % 2]) for i in range(devices)]
        return lax.ppermute(values, ALL, pairs)

    def add(left, right):
        return lax.optimization_barrier((left.astype(F32) + right.astype(F32)).astype(LINK))

    mask = tile_mask.T
    send, held, masked = partial_hidden(carried, counts, mask, neighbours, peak_weight)
    held = add(held, exchange(send, (n_peak, n_peak)))
    held, w_in, w_out, gain = lax.optimization_barrier((held, w_in, w_out, gain))
    gain = gain.reshape(1, -1)
    turned = turn(masked)
    steps = flips(n_grp, n_peak)
    for at, bits in enumerate(steps):
        held = add(held, exchange(held, tuple(bit ^ n_peak for bit in bits)))
        if at == len(steps) // 2:
            held, turned = lax.optimization_barrier((held, turned))
    other = exchange(held, (n_peak, n_peak)).astype(F32)
    held = held.astype(F32)
    lists = () if carried else (lax.all_gather(neighbours, ALL, axis=0, tiled=True).T,)
    peak_grad, gain_grad, in_grad, out_grad = tower(
        carried, length_of, held, other, turned, gain, w_in, w_out, *lists
    )
    return (peak_grad, gain_grad.reshape(-1), in_grad, out_grad)


def solution(mesh):
    placed = (
        P(None, ALL),
        P(None, ALL),
        P(ALL, None),
        P(ALL, None),
        P(),
        P(),
        P(),
    )
    return jax.shard_map(
        functools.partial(body, mesh.shape["grp"], mesh.shape["peak"]),
        mesh=mesh,
        in_specs=placed,
        out_specs=(P(ALL, None), P(), P(), P()),
        check_vma=False,
    )
```

```python
import functools

import jax
import jax.numpy as jnp
from jax import lax
from jax.experimental import pallas as pl
from jax.experimental.pallas import tpu as pltpu
from jax.sharding import PartitionSpec as P

TILE = 128
SLOTS = 8
ALL = ("grp", "peak")
MIB = 1024 * 1024
F32 = jnp.float32
BF16 = jnp.bfloat16
LINK = jnp.float16
LIFT = 2.0

sharpness_divisor = 0.2
eps_norm = 1e-06
gelu_coef = 0.7978845608
cubic_coef = 0.044715


def dot(left, right, left_dim, right_dim):
    return lax.dot_general(
        left, right, (((left_dim,), (right_dim,)), ((), ())), preferred_element_type=F32
    )


def place():
    return lax.axis_index("grp") * lax.axis_size("peak") + lax.axis_index("peak")


def own_half():
    position = place()
    ones = position
    for bit in range(1, (lax.axis_size("grp") * lax.axis_size("peak")).bit_length()):
        ones = ones + lax.shift_right_logical(position, bit)
    return lax.rem(ones, 2)


def tiles_of(rows, columns):
    return rows // 8 * (columns // TILE)


def to_tiles(values):
    rows, columns = values.shape
    return [values[:, start : start + TILE].reshape(rows // 8, 8, TILE) for start in range(0, columns, TILE)]


def partial_kernel(
    carried, pieces, counts_hbm, mask_hbm, lists_hbm, weight_hbm, send_ref, keep_ref, masked_ref,
    counts_ref, mask_ref, lists_ref, weight_ref, total_ref, counts_sem, weight_sem, side_sem,
):
    cells, peaks = counts_ref.shape
    half = cells // 2
    span = peaks // pieces

    def copies(piece):
        at = pl.ds(piece * span, span)
        return (
            pltpu.make_async_copy(counts_hbm.at[:, at], counts_ref.at[:, at], counts_sem.at[piece]),
            pltpu.make_async_copy(weight_hbm.at[at, :], weight_ref.at[at, :], weight_sem.at[piece]),
        )

    sides = (
        pltpu.make_async_copy(mask_hbm, mask_ref, side_sem.at[0]),
        pltpu.make_async_copy(lists_hbm, lists_ref, side_sem.at[1]),
    )
    for copy in sides:
        copy.start()
    for piece in range(pieces):
        for copy in copies(piece):
            copy.start()
    for copy in sides:
        copy.wait()
    mine = own_half()
    if carried:
        own, length = lists_ref.shape
        columns = lax.broadcasted_iota(jnp.int32, (own, cells), 1)
        rows = lax.broadcasted_iota(jnp.int32, (own, cells), 0)
        lists = dot(lists_ref[...].astype(F32), (columns == rows + place() * own).astype(F32), 0, 0)
        lists = jnp.concatenate([lists, jnp.zeros((2 * SLOTS - length, cells), F32)], axis=0)
        low, high = lists[:SLOTS], lists[SLOTS:]
        first = tiles_of(half, total_ref.shape[1])
        for at, (low_tile, high_tile) in enumerate(zip(to_tiles(low), to_tiles(high), strict=True), first):
            keep_ref[at : at + 1] = jnp.where(mine == 0, low_tile, high_tile)
            send_ref[at : at + 1] = jnp.where(mine == 0, high_tile, low_tile)
    mask = mask_ref[...].astype(F32).T
    for piece in range(pieces):
        for copy in copies(piece):
            copy.wait()
        first = piece * span
        for start in range(first, first + span, TILE):
            tile = start // TILE
            column = jnp.broadcast_to(mask[:, tile : tile + 1], (cells, TILE)).astype(BF16)
            masked_ref[:, start : start + TILE] = counts_ref[:, start : start + TILE] * column
        at = slice(first, first + span)
        term = jnp.dot(masked_ref[:, at], weight_ref[at, :], preferred_element_type=F32)
        total_ref[...] = term if piece == 0 else total_ref[...] + term
    for ref, side in ((send_ref, 1 - mine), (keep_ref, mine)):
        for at, tiles in enumerate(to_tiles(LIFT * total_ref[pl.ds(side * half, half), :])):
            ref[at * (half // 8) : (at + 1) * (half // 8)] = tiles


def partial_hidden(carried, counts, mask, neighbours, peak_weight):
    cells, peaks = counts.shape
    width = peak_weight.shape[1]
    pieces = 2
    whole = pl.BlockSpec(memory_space=pltpu.VMEM)
    main = pl.BlockSpec(memory_space=pltpu.HBM)
    tiles = tiles_of(cells // 2, width) + (tiles_of(SLOTS, cells) if carried else 0)
    return pl.pallas_call(
        functools.partial(partial_kernel, carried, pieces),
        out_shape=[pltpu.VMEM((tiles, 8, TILE), F32)] * 2 + [pltpu.VMEM((cells, peaks), BF16)],
        in_specs=[main] * 4,
        out_specs=[whole] * 3,
        scratch_shapes=[
            pltpu.VMEM((cells, peaks), BF16),
            pltpu.VMEM(mask.shape, jnp.int32),
            pltpu.VMEM(neighbours.shape, jnp.int32),
            pltpu.VMEM((peaks, width), BF16),
            pltpu.VMEM((cells, width), F32),
            pltpu.SemaphoreType.DMA((pieces,)),
            pltpu.SemaphoreType.DMA((pieces,)),
            pltpu.SemaphoreType.DMA((2,)),
        ],
        compiler_params=pltpu.CompilerParams(
            vmem_limit_bytes=4 * MIB + 2 * (2 * cells * peaks + peaks * width) + 20 * cells * width
        ),
        cost_estimate=pl.CostEstimate(
            flops=2 * cells * peaks * width,
            bytes_accessed=4 * cells * peaks + 2 * peaks * width + 64 * tiles * TILE,
            transcendentals=0,
        ),
    )(*(pltpu.with_memory_space_constraint(x, pltpu.HBM) for x in (counts, mask, neighbours, peak_weight)))


def turn_kernel(masked_ref, turned_ref):
    for start in range(0, masked_ref.shape[1], TILE):
        turned_ref[start : start + TILE, :] = masked_ref[:, start : start + TILE].T


def turn(masked):
    cells, peaks = masked.shape
    whole = pl.BlockSpec(memory_space=pltpu.VMEM)
    return pl.pallas_call(
        turn_kernel,
        out_shape=pltpu.VMEM((peaks, cells), BF16),
        in_specs=[whole],
        out_specs=whole,
        compiler_params=pltpu.CompilerParams(vmem_limit_bytes=4 * MIB + 6 * cells * peaks),
        cost_estimate=pl.CostEstimate(
            flops=cells * peaks, bytes_accessed=4 * cells * peaks, transcendentals=0
        ),
    )(pltpu.with_memory_space_constraint(masked, pltpu.VMEM))


def tower_kernel(
    carried, length_of, pieces, own_ref, other_ref, turned_ref, gain_ref, w_in_ref, w_out_ref, *refs
):
    lists_refs, refs = ((), refs) if carried else (refs[:1], refs[1:])
    peak_grad_hbm, gain_grad_hbm, in_grad_hbm, out_grad_hbm, *refs = refs
    hidden_ref, peak_grad_ref, gain_grad_ref, in_grad_ref, out_grad_ref, peak_sem, side_sem = refs
    cells = hidden_ref.shape[0]
    half = cells // 2
    gain_copy = pltpu.make_async_copy(gain_grad_ref, gain_grad_hbm, side_sem.at[0])
    in_copy = pltpu.make_async_copy(in_grad_ref, in_grad_hbm, side_sem.at[1])
    out_copy = pltpu.make_async_copy(out_grad_ref, out_grad_hbm, side_sem.at[2])
    mine = own_half()
    for ref, side in ((own_ref, mine), (other_ref, 1 - mine)):
        for at in range(hidden_ref.shape[1] // TILE):
            tiles = ref[at * (half // 8) : (at + 1) * (half // 8)]
            hidden_ref[pl.ds(side * half, half), at * TILE : (at + 1) * TILE] = tiles.reshape(half, TILE) * (1.0 / LIFT)
    if carried:
        first = tiles_of(half, hidden_ref.shape[1])
        pairs = [(own_ref[at], other_ref[at]) for at in range(first, own_ref.shape[0])]
        low = [jnp.where(mine == 0, own, other) for own, other in pairs]
        high = [jnp.where(mine == 0, other, own) for own, other in pairs]
        lists = jnp.concatenate([jnp.concatenate(low, axis=1), jnp.concatenate(high, axis=1)], axis=0)
    else:
        lists = lists_refs[0][...].astype(F32)
    gain = gain_ref[...]
    w_in, w_out = w_in_ref[...], w_out_ref[...]

    hidden = hidden_ref[...]
    scale = lax.rsqrt(jnp.mean(hidden * hidden, axis=1, keepdims=True) + eps_norm)
    normed = hidden * scale
    rounded = (normed * gain).astype(BF16)
    preact = jnp.dot(rounded, w_in, preferred_element_type=F32)
    square = preact * preact
    tangent = jnp.tanh(gelu_coef * preact * (1.0 + cubic_coef * square))
    activ = (0.5 * preact * (1.0 + tangent)).astype(BF16)
    slope = 0.5 * (1.0 + tangent) + 0.5 * preact * (1.0 - tangent * tangent) * gelu_coef * (
        1.0 + 3.0 * cubic_coef * square
    )
    project = jnp.dot(activ, w_out, preferred_element_type=F32)
    length = lax.rsqrt(jnp.sum(project * project, axis=1, keepdims=True) + eps_norm)
    unit = project * length
    codes = unit.astype(BF16)

    scores = dot(codes, codes, 1, 1) / sharpness_divisor
    targets = lax.broadcasted_iota(jnp.int32, (cells, cells), 0)
    sources = lax.broadcasted_iota(jnp.int32, (cells, cells), 1)
    expo = jnp.where(targets == sources, 0.0, jnp.exp(scores))
    prob = expo * (1.0 / jnp.sum(expo, axis=0, keepdims=True))
    places = targets.astype(F32)
    tallies = jnp.zeros((cells, cells), F32)
    for slot in range(length_of):
        tallies = tallies + (lists[slot : slot + 1] == places).astype(F32)
    coupling = (prob - tallies / length_of).astype(BF16)
    dcodes = (dot(coupling, codes, 0, 0) + dot(coupling, codes, 1, 0)) / sharpness_divisor

    dproj = (length * (dcodes - unit * jnp.sum(unit * dcodes, axis=1, keepdims=True))).astype(BF16)
    dpre = (dot(dproj, w_out, 1, 1) * slope).astype(BF16)
    out_grad_ref[...] = dot(activ, dproj, 0, 0)
    out_copy.start()
    dround = dot(dpre, w_in, 1, 1)
    in_grad_ref[...] = dot(rounded, dpre, 0, 0)
    in_copy.start()
    gain_grad_ref[...] = jnp.sum(dround * normed, axis=0, keepdims=True)
    gain_copy.start()
    dnorm = dround * gain
    dhidden = (scale * (dnorm - normed * jnp.mean(dnorm * normed, axis=1, keepdims=True))).astype(BF16)

    span = turned_ref.shape[0] // pieces

    def peak_copy(piece):
        at = pl.ds(piece * span, span)
        return pltpu.make_async_copy(peak_grad_ref.at[at, :], peak_grad_hbm.at[at, :], peak_sem.at[piece])

    @pl.loop(0, 2)
    def _(part):
        for inner in range(pieces // 2):
            piece = part * (pieces // 2) + inner
            at = pl.ds(pl.multiple_of(piece * span, span), span)
            peak_grad_ref[at, :] = jnp.dot(turned_ref[at, :], dhidden, preferred_element_type=F32)
            peak_copy(piece).start()

    for piece in range(pieces):
        peak_copy(piece).wait()
    gain_copy.wait()
    in_copy.wait()
    out_copy.wait()


def tower(carried, length_of, own, other, turned, gain, w_in, w_out, *lists):
    peaks, cells = turned.shape
    width, hid = w_in.shape
    codes = w_out.shape[1]
    pieces = 4
    whole = pl.BlockSpec(memory_space=pltpu.VMEM)
    main = pl.BlockSpec(memory_space=pltpu.HBM)
    return pl.pallas_call(
        functools.partial(tower_kernel, carried, length_of, pieces),
        out_shape=[
            jax.ShapeDtypeStruct((peaks, width), F32),
            jax.ShapeDtypeStruct((1, width), F32),
            jax.ShapeDtypeStruct((width, hid), F32),
            jax.ShapeDtypeStruct((hid, codes), F32),
        ],
        in_specs=[whole] * (6 + len(lists)),
        out_specs=[main] * 4,
        scratch_shapes=[
            pltpu.VMEM((cells, width), F32),
            pltpu.VMEM((peaks, width), F32),
            pltpu.VMEM((1, width), F32),
            pltpu.VMEM((width, hid), F32),
            pltpu.VMEM((hid, codes), F32),
            pltpu.SemaphoreType.DMA((pieces,)),
            pltpu.SemaphoreType.DMA((3,)),
        ],
        compiler_params=pltpu.CompilerParams(
            vmem_limit_bytes=min(
                56 * MIB,
                4 * (MIB + peaks * width + width * hid + hid * codes) + cells * (64 * width + 20 * cells),
            )
        ),
        cost_estimate=pl.CostEstimate(
            flops=2 * cells * width * (peaks + 3 * hid + 3 * codes),
            bytes_accessed=2 * peaks * cells + 4 * peaks * width + 6 * width * hid + 6 * hid * codes,
            transcendentals=cells * (hid + cells),
        ),
    )(own, other, turned, gain, w_in, w_out, *lists)


def chip_steps(n_grp, n_peak):
    grp_bits = [bit * n_peak for bit in (2, 4, 8, 16, 32, 64) if bit < n_grp]
    peak_bits = [bit for bit in (1, 2, 4, 8, 16, 32, 64) if bit < n_peak]
    order = grp_bits + peak_bits
    fours = [(min(pair), max(pair), sum(pair)) for pair in zip(order[::2], order[1::2], strict=False)]
    steps = [list(zip(*both, strict=True)) for both in zip(reversed(fours), fours, strict=True)]
    return steps + [[(bit, bit)] for bit in order[2 * len(fours) :]]


def body(n_grp, n_peak, counts, tile_mask, neighbours, peak_weight, gain, w_in, w_out):
    cells = counts.shape[0]
    length_of = neighbours.shape[1]
    carried = cells <= 512 and length_of <= 2 * SLOTS
    devices = n_grp * n_peak

    def exchange(values, bits):
        def partner(i):
            bit = bits[i.bit_count() % 2]
            return i ^ bit ^ (n_peak if bit.bit_count() % 2 else 0)

        return lax.ppermute(values, ALL, [(i, partner(i)) for i in range(devices)])

    def between_cores(values):
        return lax.ppermute(values, ALL, [(i, i ^ n_peak) for i in range(devices)])

    def total(terms):
        terms = [term.astype(F32) for term in terms]
        while len(terms) > 1:
            terms = [left + right for left, right in zip(terms[::2], terms[1::2], strict=True)]
        return lax.optimization_barrier(terms[0].astype(LINK))

    mask = tile_mask.T
    send, held, masked = partial_hidden(carried, counts, mask, neighbours, peak_weight)
    held = total([held, between_cores(send)])
    held, w_in, w_out, gain = lax.optimization_barrier((held, w_in, w_out, gain))
    gain = gain.reshape(1, -1)
    turned = turn(masked)
    steps = chip_steps(n_grp, n_peak)
    for step in steps:
        held = total([held] + [exchange(held, bits) for bits in step])
        if step is steps[-1]:
            held, turned = lax.optimization_barrier((held, turned))
    other = between_cores(held).astype(F32)
    held = held.astype(F32)
    lists = () if carried else (lax.all_gather(neighbours, ALL, axis=0, tiled=True).T,)
    peak_grad, gain_grad, in_grad, out_grad = tower(
        carried, length_of, held, other, turned, gain, w_in, w_out, *lists
    )
    return (peak_grad, gain_grad.reshape(-1), in_grad, out_grad)


def solution(mesh):
    placed = (
        P(None, ALL),
        P(None, ALL),
        P(ALL, None),
        P(ALL, None),
        P(),
        P(),
        P(),
    )
    return jax.shard_map(
        functools.partial(body, mesh.shape["grp"], mesh.shape["peak"]),
        mesh=mesh,
        in_specs=placed,
        out_specs=(P(ALL, None), P(), P(), P()),
        check_vma=False,
    )
```

```python
import functools

import jax
import jax.numpy as jnp
from jax import lax
from jax.experimental import pallas as pl
from jax.experimental.pallas import tpu as pltpu
from jax.sharding import PartitionSpec as P

TILE = 128
SLOTS = 8
ALL = ("grp", "peak")
MIB = 1024 * 1024
F32 = jnp.float32
BF16 = jnp.bfloat16
LINK = jnp.float16
LIFT = 2.0

sharpness_divisor = 0.2
eps_norm = 1e-06
gelu_coef = 0.7978845608
cubic_coef = 0.044715


def dot(left, right, left_dim, right_dim):
    return lax.dot_general(
        left, right, (((left_dim,), (right_dim,)), ((), ())), preferred_element_type=F32
    )


def place():
    return lax.axis_index("grp") * lax.axis_size("peak") + lax.axis_index("peak")


def own_half():
    position = place()
    ones = position
    for bit in range(1, (lax.axis_size("grp") * lax.axis_size("peak")).bit_length()):
        ones = ones + lax.shift_right_logical(position, bit)
    return lax.rem(ones, 2)


def tiles_of(rows, columns):
    return rows // 8 * (columns // TILE)


def to_tiles(values):
    rows, columns = values.shape
    return [values[:, start : start + TILE].reshape(rows // 8, 8, TILE) for start in range(0, columns, TILE)]


def partial_kernel(
    carried, pieces, counts_hbm, mask_hbm, lists_hbm, weight_hbm, send_ref, keep_ref, masked_ref,
    counts_ref, mask_ref, lists_ref, weight_ref, total_ref, counts_sem, weight_sem, side_sem,
):
    cells, peaks = counts_ref.shape
    half = cells // 2
    span = peaks // pieces

    def copies(piece):
        at = pl.ds(piece * span, span)
        return (
            pltpu.make_async_copy(counts_hbm.at[:, at], counts_ref.at[:, at], counts_sem.at[piece]),
            pltpu.make_async_copy(weight_hbm.at[at, :], weight_ref.at[at, :], weight_sem.at[piece]),
        )

    sides = (
        pltpu.make_async_copy(mask_hbm, mask_ref, side_sem.at[0]),
        pltpu.make_async_copy(lists_hbm, lists_ref, side_sem.at[1]),
    )
    for copy in sides:
        copy.start()
    for piece in range(pieces):
        for copy in copies(piece):
            copy.start()
    for copy in sides:
        copy.wait()
    mine = own_half()
    if carried:
        own, length = lists_ref.shape
        columns = lax.broadcasted_iota(jnp.int32, (own, cells), 1)
        rows = lax.broadcasted_iota(jnp.int32, (own, cells), 0)
        lists = dot(lists_ref[...].astype(F32), (columns == rows + place() * own).astype(F32), 0, 0)
        lists = jnp.concatenate([lists, jnp.zeros((2 * SLOTS - length, cells), F32)], axis=0)
        low, high = lists[:SLOTS], lists[SLOTS:]
        first = tiles_of(half, total_ref.shape[1])
        for at, (low_tile, high_tile) in enumerate(zip(to_tiles(low), to_tiles(high), strict=True), first):
            keep_ref[at : at + 1] = jnp.where(mine == 0, low_tile, high_tile)
            send_ref[at : at + 1] = jnp.where(mine == 0, high_tile, low_tile)
    mask = mask_ref[...].astype(F32).T
    for piece in range(pieces):
        for copy in copies(piece):
            copy.wait()
        first = piece * span
        for start in range(first, first + span, TILE):
            tile = start // TILE
            column = jnp.broadcast_to(mask[:, tile : tile + 1], (cells, TILE)).astype(BF16)
            masked_ref[:, start : start + TILE] = counts_ref[:, start : start + TILE] * column
        at = slice(first, first + span)
        term = jnp.dot(masked_ref[:, at], weight_ref[at, :], preferred_element_type=F32)
        total_ref[...] = term if piece == 0 else total_ref[...] + term
    for ref, side in ((send_ref, 1 - mine), (keep_ref, mine)):
        for at, tiles in enumerate(to_tiles(LIFT * total_ref[pl.ds(side * half, half), :])):
            ref[at * (half // 8) : (at + 1) * (half // 8)] = tiles


def partial_hidden(carried, counts, mask, neighbours, peak_weight):
    cells, peaks = counts.shape
    width = peak_weight.shape[1]
    pieces = 2
    whole = pl.BlockSpec(memory_space=pltpu.VMEM)
    main = pl.BlockSpec(memory_space=pltpu.HBM)
    tiles = tiles_of(cells // 2, width) + (tiles_of(SLOTS, cells) if carried else 0)
    return pl.pallas_call(
        functools.partial(partial_kernel, carried, pieces),
        out_shape=[pltpu.VMEM((tiles, 8, TILE), F32)] * 2 + [pltpu.VMEM((cells, peaks), BF16)],
        in_specs=[main] * 4,
        out_specs=[whole] * 3,
        scratch_shapes=[
            pltpu.VMEM((cells, peaks), BF16),
            pltpu.VMEM(mask.shape, jnp.int32),
            pltpu.VMEM(neighbours.shape, jnp.int32),
            pltpu.VMEM((peaks, width), BF16),
            pltpu.VMEM((cells, width), F32),
            pltpu.SemaphoreType.DMA((pieces,)),
            pltpu.SemaphoreType.DMA((pieces,)),
            pltpu.SemaphoreType.DMA((2,)),
        ],
        compiler_params=pltpu.CompilerParams(
            vmem_limit_bytes=4 * MIB + 2 * (2 * cells * peaks + peaks * width) + 20 * cells * width
        ),
        cost_estimate=pl.CostEstimate(
            flops=2 * cells * peaks * width,
            bytes_accessed=4 * cells * peaks + 2 * peaks * width + 64 * tiles * TILE,
            transcendentals=0,
        ),
    )(*(pltpu.with_memory_space_constraint(x, pltpu.HBM) for x in (counts, mask, neighbours, peak_weight)))


def turn_kernel(masked_ref, turned_ref):
    for start in range(0, masked_ref.shape[1], TILE):
        turned_ref[start : start + TILE, :] = masked_ref[:, start : start + TILE].T


def turn(masked):
    cells, peaks = masked.shape
    whole = pl.BlockSpec(memory_space=pltpu.VMEM)
    return pl.pallas_call(
        turn_kernel,
        out_shape=pltpu.VMEM((peaks, cells), BF16),
        in_specs=[whole],
        out_specs=whole,
        compiler_params=pltpu.CompilerParams(vmem_limit_bytes=4 * MIB + 6 * cells * peaks),
        cost_estimate=pl.CostEstimate(
            flops=cells * peaks, bytes_accessed=4 * cells * peaks, transcendentals=0
        ),
    )(pltpu.with_memory_space_constraint(masked, pltpu.VMEM))


def tower_kernel(
    carried, length_of, pieces, own_ref, other_ref, turned_ref, gain_ref, w_in_ref, w_out_ref, *refs
):
    lists_refs, refs = ((), refs) if carried else (refs[:1], refs[1:])
    peak_grad_hbm, gain_grad_hbm, in_grad_hbm, out_grad_hbm, *refs = refs
    hidden_ref, peak_grad_ref, gain_grad_ref, in_grad_ref, out_grad_ref, peak_sem, side_sem = refs
    cells = hidden_ref.shape[0]
    half = cells // 2
    gain_copy = pltpu.make_async_copy(gain_grad_ref, gain_grad_hbm, side_sem.at[0])
    in_copy = pltpu.make_async_copy(in_grad_ref, in_grad_hbm, side_sem.at[1])
    out_copy = pltpu.make_async_copy(out_grad_ref, out_grad_hbm, side_sem.at[2])
    mine = own_half()
    for ref, side in ((own_ref, mine), (other_ref, 1 - mine)):
        for at in range(hidden_ref.shape[1] // TILE):
            tiles = ref[at * (half // 8) : (at + 1) * (half // 8)]
            hidden_ref[pl.ds(side * half, half), at * TILE : (at + 1) * TILE] = tiles.reshape(half, TILE) * (1.0 / LIFT)
    if carried:
        first = tiles_of(half, hidden_ref.shape[1])
        pairs = [(own_ref[at], other_ref[at]) for at in range(first, own_ref.shape[0])]
        low = [jnp.where(mine == 0, own, other) for own, other in pairs]
        high = [jnp.where(mine == 0, other, own) for own, other in pairs]
        lists = jnp.concatenate([jnp.concatenate(low, axis=1), jnp.concatenate(high, axis=1)], axis=0)
    else:
        lists = lists_refs[0][...].astype(F32)
    gain = gain_ref[...]
    w_in, w_out = w_in_ref[...], w_out_ref[...]

    hidden = hidden_ref[...]
    scale = lax.rsqrt(jnp.mean(hidden * hidden, axis=1, keepdims=True) + eps_norm)
    normed = hidden * scale
    rounded = (normed * gain).astype(BF16)
    preact = jnp.dot(rounded, w_in, preferred_element_type=F32)
    square = preact * preact
    tangent = jnp.tanh(gelu_coef * preact * (1.0 + cubic_coef * square))
    activ = (0.5 * preact * (1.0 + tangent)).astype(BF16)
    slope = 0.5 * (1.0 + tangent) + 0.5 * preact * (1.0 - tangent * tangent) * gelu_coef * (
        1.0 + 3.0 * cubic_coef * square
    )
    project = jnp.dot(activ, w_out, preferred_element_type=F32)
    length = lax.rsqrt(jnp.sum(project * project, axis=1, keepdims=True) + eps_norm)
    unit = project * length
    codes = unit.astype(BF16)

    scores = dot(codes, codes, 1, 1) / sharpness_divisor
    targets = lax.broadcasted_iota(jnp.int32, (cells, cells), 0)
    sources = lax.broadcasted_iota(jnp.int32, (cells, cells), 1)
    expo = jnp.where(targets == sources, 0.0, jnp.exp(scores))
    prob = expo * (1.0 / jnp.sum(expo, axis=0, keepdims=True))
    places = targets.astype(F32)
    tallies = jnp.zeros((cells, cells), F32)
    for slot in range(length_of):
        tallies = tallies + (lists[slot : slot + 1] == places).astype(F32)
    coupling = (prob - tallies / length_of).astype(BF16)
    dcodes = (dot(coupling, codes, 0, 0) + dot(coupling, codes, 1, 0)) / sharpness_divisor

    dproj = (length * (dcodes - unit * jnp.sum(unit * dcodes, axis=1, keepdims=True))).astype(BF16)
    dpre = (dot(dproj, w_out, 1, 1) * slope).astype(BF16)
    out_grad_ref[...] = dot(activ, dproj, 0, 0)
    out_copy.start()
    dround = dot(dpre, w_in, 1, 1)
    in_grad_ref[...] = dot(rounded, dpre, 0, 0)
    in_copy.start()
    gain_grad_ref[...] = jnp.sum(dround * normed, axis=0, keepdims=True)
    gain_copy.start()
    dnorm = dround * gain
    dhidden = (scale * (dnorm - normed * jnp.mean(dnorm * normed, axis=1, keepdims=True))).astype(BF16)

    span = turned_ref.shape[0] // pieces

    def peak_copy(piece):
        at = pl.ds(piece * span, span)
        return pltpu.make_async_copy(peak_grad_ref.at[at, :], peak_grad_hbm.at[at, :], peak_sem.at[piece])

    @pl.loop(0, 2)
    def _(part):
        for inner in range(pieces // 2):
            piece = part * (pieces // 2) + inner
            at = pl.ds(pl.multiple_of(piece * span, span), span)
            peak_grad_ref[at, :] = jnp.dot(turned_ref[at, :], dhidden, preferred_element_type=F32)
            peak_copy(piece).start()

    for piece in range(pieces):
        peak_copy(piece).wait()
    gain_copy.wait()
    in_copy.wait()
    out_copy.wait()


def tower(carried, length_of, own, other, turned, gain, w_in, w_out, *lists):
    peaks, cells = turned.shape
    width, hid = w_in.shape
    codes = w_out.shape[1]
    pieces = 4
    whole = pl.BlockSpec(memory_space=pltpu.VMEM)
    main = pl.BlockSpec(memory_space=pltpu.HBM)
    return pl.pallas_call(
        functools.partial(tower_kernel, carried, length_of, pieces),
        out_shape=[
            jax.ShapeDtypeStruct((peaks, width), F32),
            jax.ShapeDtypeStruct((1, width), F32),
            jax.ShapeDtypeStruct((width, hid), F32),
            jax.ShapeDtypeStruct((hid, codes), F32),
        ],
        in_specs=[whole] * (6 + len(lists)),
        out_specs=[main] * 4,
        scratch_shapes=[
            pltpu.VMEM((cells, width), F32),
            pltpu.VMEM((peaks, width), F32),
            pltpu.VMEM((1, width), F32),
            pltpu.VMEM((width, hid), F32),
            pltpu.VMEM((hid, codes), F32),
            pltpu.SemaphoreType.DMA((pieces,)),
            pltpu.SemaphoreType.DMA((3,)),
        ],
        compiler_params=pltpu.CompilerParams(
            vmem_limit_bytes=min(
                56 * MIB,
                4 * (MIB + peaks * width + width * hid + hid * codes) + cells * (64 * width + 20 * cells),
            )
        ),
        cost_estimate=pl.CostEstimate(
            flops=2 * cells * width * (peaks + 3 * hid + 3 * codes),
            bytes_accessed=2 * peaks * cells + 4 * peaks * width + 6 * width * hid + 6 * hid * codes,
            transcendentals=cells * (hid + cells),
        ),
    )(own, other, turned, gain, w_in, w_out, *lists)


def chip_steps(n_grp, n_peak):
    grp_bits = [bit * n_peak for bit in (2, 4, 8, 16, 32, 64) if bit < n_grp]
    peak_bits = [bit for bit in (1, 2, 4, 8, 16, 32, 64) if bit < n_peak]
    order = grp_bits + peak_bits
    fours = [(min(pair), max(pair), sum(pair)) for pair in zip(order[::2], order[1::2], strict=False)]
    steps = [list(zip(*both, strict=True)) for both in zip(reversed(fours), fours, strict=True)]
    return steps + [[(bit, bit)] for bit in order[2 * len(fours) :]]


def body(n_grp, n_peak, counts, tile_mask, neighbours, peak_weight, gain, w_in, w_out):
    cells = counts.shape[0]
    length_of = neighbours.shape[1]
    carried = cells <= 512 and length_of <= 2 * SLOTS
    devices = n_grp * n_peak

    def exchange(values, bits):
        def partner(i):
            bit = bits[i.bit_count() % 2]
            return i ^ bit ^ (n_peak if bit.bit_count() % 2 else 0)

        return lax.ppermute(values, ALL, [(i, partner(i)) for i in range(devices)])

    def between_cores(values):
        return lax.ppermute(values, ALL, [(i, i ^ n_peak) for i in range(devices)])

    def total(terms):
        terms = [term.astype(F32) for term in terms]
        while len(terms) > 1:
            terms = [left + right for left, right in zip(terms[::2], terms[1::2], strict=True)]
        return lax.optimization_barrier(terms[0].astype(LINK))

    mask = tile_mask.T
    send, held, masked = partial_hidden(carried, counts, mask, neighbours, peak_weight)
    held = total([held, between_cores(lax.optimization_barrier(send.astype(LINK)))])
    held, w_in, w_out, gain = lax.optimization_barrier((held, w_in, w_out, gain))
    gain = gain.reshape(1, -1)
    turned = turn(masked)
    steps = chip_steps(n_grp, n_peak)
    for step in steps:
        held = total([held] + [exchange(held, bits) for bits in step])
        if step is steps[-1]:
            held, turned = lax.optimization_barrier((held, turned))
    other = between_cores(held).astype(F32)
    held = held.astype(F32)
    lists = () if carried else (lax.all_gather(neighbours, ALL, axis=0, tiled=True).T,)
    peak_grad, gain_grad, in_grad, out_grad = tower(
        carried, length_of, held, other, turned, gain, w_in, w_out, *lists
    )
    return (peak_grad, gain_grad.reshape(-1), in_grad, out_grad)


def solution(mesh):
    placed = (
        P(None, ALL),
        P(None, ALL),
        P(ALL, None),
        P(ALL, None),
        P(),
        P(),
        P(),
    )
    return jax.shard_map(
        functools.partial(body, mesh.shape["grp"], mesh.shape["peak"]),
        mesh=mesh,
        in_specs=placed,
        out_specs=(P(ALL, None), P(), P(), P()),
        check_vma=False,
    )
```

```python
import functools

import jax
import jax.numpy as jnp
from jax import lax
from jax.experimental import pallas as pl
from jax.experimental.pallas import tpu as pltpu
from jax.sharding import PartitionSpec as P

TILE = 128
SLOTS = 8
ALL = ("grp", "peak")
MIB = 1024 * 1024
F32 = jnp.float32
BF16 = jnp.bfloat16
LINK = jnp.float16
LIFT = 2.0

sharpness_divisor = 0.2
eps_norm = 1e-06
gelu_coef = 0.7978845608
cubic_coef = 0.044715


def dot(left, right, left_dim, right_dim):
    return lax.dot_general(
        left, right, (((left_dim,), (right_dim,)), ((), ())), preferred_element_type=F32
    )


def place():
    return lax.axis_index("grp") * lax.axis_size("peak") + lax.axis_index("peak")


def own_half():
    position = place()
    ones = position
    for bit in range(1, (lax.axis_size("grp") * lax.axis_size("peak")).bit_length()):
        ones = ones + lax.shift_right_logical(position, bit)
    return lax.rem(ones, 2)


def tiles_of(rows, columns):
    return rows // 8 * (columns // TILE)


def to_tiles(values):
    rows, columns = values.shape
    return [values[:, start : start + TILE].reshape(rows // 8, 8, TILE) for start in range(0, columns, TILE)]


def partial_kernel(
    carried, pieces, counts_hbm, mask_hbm, lists_hbm, weight_hbm, send_ref, keep_ref, masked_ref,
    counts_ref, mask_ref, lists_ref, weight_ref, total_ref, counts_sem, weight_sem, side_sem,
):
    cells, peaks = counts_ref.shape
    half = cells // 2
    span = peaks // pieces

    def copies(piece):
        at = pl.ds(piece * span, span)
        return (
            pltpu.make_async_copy(counts_hbm.at[:, at], counts_ref.at[:, at], counts_sem.at[piece]),
            pltpu.make_async_copy(weight_hbm.at[at, :], weight_ref.at[at, :], weight_sem.at[piece]),
        )

    sides = (
        pltpu.make_async_copy(mask_hbm, mask_ref, side_sem.at[0]),
        pltpu.make_async_copy(lists_hbm, lists_ref, side_sem.at[1]),
    )
    for copy in sides:
        copy.start()
    for piece in range(pieces):
        for copy in copies(piece):
            copy.start()
    for copy in sides:
        copy.wait()
    mine = own_half()
    if carried:
        own, length = lists_ref.shape
        columns = lax.broadcasted_iota(jnp.int32, (own, cells), 1)
        rows = lax.broadcasted_iota(jnp.int32, (own, cells), 0)
        lists = dot(lists_ref[...].astype(F32), (columns == rows + place() * own).astype(F32), 0, 0)
        lists = jnp.concatenate([lists, jnp.zeros((2 * SLOTS - length, cells), F32)], axis=0)
        low, high = lists[:SLOTS], lists[SLOTS:]
        first = tiles_of(half, total_ref.shape[1])
        for at, (low_tile, high_tile) in enumerate(zip(to_tiles(low), to_tiles(high), strict=True), first):
            keep_ref[at : at + 1] = jnp.where(mine == 0, low_tile, high_tile)
            send_ref[at : at + 1] = jnp.where(mine == 0, high_tile, low_tile)
    mask = mask_ref[...].astype(F32).T
    for piece in range(pieces):
        for copy in copies(piece):
            copy.wait()
        first = piece * span
        for start in range(first, first + span, TILE):
            tile = start // TILE
            column = jnp.broadcast_to(mask[:, tile : tile + 1], (cells, TILE)).astype(BF16)
            masked_ref[:, start : start + TILE] = counts_ref[:, start : start + TILE] * column
        at = slice(first, first + span)
        term = jnp.dot(masked_ref[:, at], weight_ref[at, :], preferred_element_type=F32)
        total_ref[...] = term if piece == 0 else total_ref[...] + term
    for ref, side in ((send_ref, 1 - mine), (keep_ref, mine)):
        for at, tiles in enumerate(to_tiles(LIFT * total_ref[pl.ds(side * half, half), :])):
            ref[at * (half // 8) : (at + 1) * (half // 8)] = tiles


def partial_hidden(carried, counts, mask, neighbours, peak_weight):
    cells, peaks = counts.shape
    width = peak_weight.shape[1]
    pieces = 2
    whole = pl.BlockSpec(memory_space=pltpu.VMEM)
    main = pl.BlockSpec(memory_space=pltpu.HBM)
    tiles = tiles_of(cells // 2, width) + (tiles_of(SLOTS, cells) if carried else 0)
    return pl.pallas_call(
        functools.partial(partial_kernel, carried, pieces),
        out_shape=[pltpu.VMEM((tiles, 8, TILE), F32)] * 2 + [pltpu.VMEM((cells, peaks), BF16)],
        in_specs=[main] * 4,
        out_specs=[whole] * 3,
        scratch_shapes=[
            pltpu.VMEM((cells, peaks), BF16),
            pltpu.VMEM(mask.shape, jnp.int32),
            pltpu.VMEM(neighbours.shape, jnp.int32),
            pltpu.VMEM((peaks, width), BF16),
            pltpu.VMEM((cells, width), F32),
            pltpu.SemaphoreType.DMA((pieces,)),
            pltpu.SemaphoreType.DMA((pieces,)),
            pltpu.SemaphoreType.DMA((2,)),
        ],
        compiler_params=pltpu.CompilerParams(
            vmem_limit_bytes=4 * MIB + 2 * (2 * cells * peaks + peaks * width) + 20 * cells * width
        ),
        cost_estimate=pl.CostEstimate(
            flops=2 * cells * peaks * width,
            bytes_accessed=4 * cells * peaks + 2 * peaks * width + 64 * tiles * TILE,
            transcendentals=0,
        ),
    )(*(pltpu.with_memory_space_constraint(x, pltpu.HBM) for x in (counts, mask, neighbours, peak_weight)))


def turn_kernel(masked_ref, turned_ref):
    for start in range(0, masked_ref.shape[1], TILE):
        turned_ref[start : start + TILE, :] = masked_ref[:, start : start + TILE].T


def turn(masked):
    cells, peaks = masked.shape
    whole = pl.BlockSpec(memory_space=pltpu.VMEM)
    return pl.pallas_call(
        turn_kernel,
        out_shape=pltpu.VMEM((peaks, cells), BF16),
        in_specs=[whole],
        out_specs=whole,
        compiler_params=pltpu.CompilerParams(vmem_limit_bytes=4 * MIB + 6 * cells * peaks),
        cost_estimate=pl.CostEstimate(
            flops=cells * peaks, bytes_accessed=4 * cells * peaks, transcendentals=0
        ),
    )(pltpu.with_memory_space_constraint(masked, pltpu.VMEM))


def tower_kernel(
    carried, length_of, pieces, own_ref, other_ref, turned_ref, gain_ref, w_in_ref, w_out_ref, *refs
):
    lists_refs, refs = ((), refs) if carried else (refs[:1], refs[1:])
    peak_grad_hbm, gain_grad_hbm, in_grad_hbm, out_grad_hbm, *refs = refs
    hidden_ref, peak_grad_ref, gain_grad_ref, in_grad_ref, out_grad_ref, peak_sem, side_sem = refs
    cells = hidden_ref.shape[0]
    half = cells // 2
    gain_copy = pltpu.make_async_copy(gain_grad_ref, gain_grad_hbm, side_sem.at[0])
    in_copy = pltpu.make_async_copy(in_grad_ref, in_grad_hbm, side_sem.at[1])
    out_copy = pltpu.make_async_copy(out_grad_ref, out_grad_hbm, side_sem.at[2])
    mine = own_half()
    for ref, side in ((own_ref, mine), (other_ref, 1 - mine)):
        for at in range(hidden_ref.shape[1] // TILE):
            tiles = ref[at * (half // 8) : (at + 1) * (half // 8)]
            hidden_ref[pl.ds(side * half, half), at * TILE : (at + 1) * TILE] = tiles.reshape(half, TILE) * (1.0 / LIFT)
    if carried:
        first = tiles_of(half, hidden_ref.shape[1])
        pairs = [(own_ref[at], other_ref[at]) for at in range(first, own_ref.shape[0])]
        low = [jnp.where(mine == 0, own, other) for own, other in pairs]
        high = [jnp.where(mine == 0, other, own) for own, other in pairs]
        lists = jnp.concatenate([jnp.concatenate(low, axis=1), jnp.concatenate(high, axis=1)], axis=0)
    else:
        lists = lists_refs[0][...].astype(F32)
    gain = gain_ref[...]
    w_in, w_out = w_in_ref[...], w_out_ref[...]

    hidden = hidden_ref[...]
    scale = lax.rsqrt(jnp.mean(hidden * hidden, axis=1, keepdims=True) + eps_norm)
    normed = hidden * scale
    rounded = (normed * gain).astype(BF16)
    preact = jnp.dot(rounded, w_in, preferred_element_type=F32)
    square = preact * preact
    tangent = jnp.tanh(gelu_coef * preact * (1.0 + cubic_coef * square))
    activ = (0.5 * preact * (1.0 + tangent)).astype(BF16)
    slope = 0.5 * (1.0 + tangent) + 0.5 * preact * (1.0 - tangent * tangent) * gelu_coef * (
        1.0 + 3.0 * cubic_coef * square
    )
    project = jnp.dot(activ, w_out, preferred_element_type=F32)
    length = lax.rsqrt(jnp.sum(project * project, axis=1, keepdims=True) + eps_norm)
    unit = project * length
    codes = unit.astype(BF16)

    scores = dot(codes, codes, 1, 1) * (1.0 / sharpness_divisor)
    targets = lax.broadcasted_iota(jnp.int32, (cells, cells), 0)
    sources = lax.broadcasted_iota(jnp.int32, (cells, cells), 1)
    expo = jnp.where(targets == sources, 0.0, jnp.exp(scores))
    prob = expo * (1.0 / jnp.sum(expo, axis=0, keepdims=True))
    places = targets.astype(F32)
    tallies = jnp.zeros((cells, cells), F32)
    for slot in range(length_of):
        tallies = tallies + (lists[slot : slot + 1] == places).astype(F32)
    coupling = (prob - tallies * (1.0 / length_of)).astype(BF16)
    dcodes = (dot(coupling, codes, 0, 0) + dot(coupling, codes, 1, 0)) * (1.0 / sharpness_divisor)

    dproj = (length * (dcodes - unit * jnp.sum(unit * dcodes, axis=1, keepdims=True))).astype(BF16)
    dpre = (dot(dproj, w_out, 1, 1) * slope).astype(BF16)
    out_grad_ref[...] = dot(activ, dproj, 0, 0)
    out_copy.start()
    dround = dot(dpre, w_in, 1, 1)
    in_grad_ref[...] = dot(rounded, dpre, 0, 0)
    in_copy.start()
    gain_grad_ref[...] = jnp.sum(dround * normed, axis=0, keepdims=True)
    gain_copy.start()
    dnorm = dround * gain
    dhidden = (scale * (dnorm - normed * jnp.mean(dnorm * normed, axis=1, keepdims=True))).astype(BF16)

    span = turned_ref.shape[0] // pieces

    def peak_copy(piece):
        at = pl.ds(piece * span, span)
        return pltpu.make_async_copy(peak_grad_ref.at[at, :], peak_grad_hbm.at[at, :], peak_sem.at[piece])

    @pl.loop(0, 2)
    def _(part):
        for inner in range(pieces // 2):
            piece = part * (pieces // 2) + inner
            at = pl.ds(pl.multiple_of(piece * span, span), span)
            peak_grad_ref[at, :] = jnp.dot(turned_ref[at, :], dhidden, preferred_element_type=F32)
            peak_copy(piece).start()

    for piece in range(pieces):
        peak_copy(piece).wait()
    gain_copy.wait()
    in_copy.wait()
    out_copy.wait()


def tower(carried, length_of, own, other, turned, gain, w_in, w_out, *lists):
    peaks, cells = turned.shape
    width, hid = w_in.shape
    codes = w_out.shape[1]
    pieces = 4
    whole = pl.BlockSpec(memory_space=pltpu.VMEM)
    main = pl.BlockSpec(memory_space=pltpu.HBM)
    return pl.pallas_call(
        functools.partial(tower_kernel, carried, length_of, pieces),
        out_shape=[
            jax.ShapeDtypeStruct((peaks, width), F32),
            jax.ShapeDtypeStruct((1, width), F32),
            jax.ShapeDtypeStruct((width, hid), F32),
            jax.ShapeDtypeStruct((hid, codes), F32),
        ],
        in_specs=[whole] * (6 + len(lists)),
        out_specs=[main] * 4,
        scratch_shapes=[
            pltpu.VMEM((cells, width), F32),
            pltpu.VMEM((peaks, width), F32),
            pltpu.VMEM((1, width), F32),
            pltpu.VMEM((width, hid), F32),
            pltpu.VMEM((hid, codes), F32),
            pltpu.SemaphoreType.DMA((pieces,)),
            pltpu.SemaphoreType.DMA((3,)),
        ],
        compiler_params=pltpu.CompilerParams(
            vmem_limit_bytes=min(
                56 * MIB,
                4 * (MIB + peaks * width + width * hid + hid * codes) + cells * (64 * width + 20 * cells),
            )
        ),
        cost_estimate=pl.CostEstimate(
            flops=2 * cells * width * (peaks + 3 * hid + 3 * codes),
            bytes_accessed=2 * peaks * cells + 4 * peaks * width + 6 * width * hid + 6 * hid * codes,
            transcendentals=cells * (hid + cells),
        ),
    )(own, other, turned, gain, w_in, w_out, *lists)


def chip_steps(n_grp, n_peak):
    grp_bits = [bit * n_peak for bit in (2, 4, 8, 16, 32, 64) if bit < n_grp]
    peak_bits = [bit for bit in (1, 2, 4, 8, 16, 32, 64) if bit < n_peak]
    order = grp_bits + peak_bits
    fours = [(min(pair), max(pair), sum(pair)) for pair in zip(order[::2], order[1::2], strict=False)]
    steps = [list(zip(*both, strict=True)) for both in zip(reversed(fours), fours, strict=True)]
    return steps + [[(bit, bit)] for bit in order[2 * len(fours) :]]


def body(n_grp, n_peak, counts, tile_mask, neighbours, peak_weight, gain, w_in, w_out):
    cells = counts.shape[0]
    length_of = neighbours.shape[1]
    carried = cells <= 512 and length_of <= 2 * SLOTS
    devices = n_grp * n_peak

    def exchange(values, bits):
        def partner(i):
            bit = bits[i.bit_count() % 2]
            return i ^ bit ^ (n_peak if bit.bit_count() % 2 else 0)

        return lax.ppermute(values, ALL, [(i, partner(i)) for i in range(devices)])

    def between_cores(values):
        return lax.ppermute(values, ALL, [(i, i ^ n_peak) for i in range(devices)])

    def total(terms):
        terms = [term.astype(F32) for term in terms]
        while len(terms) > 1:
            terms = [left + right for left, right in zip(terms[::2], terms[1::2], strict=True)]
        return lax.optimization_barrier(terms[0].astype(LINK))

    mask = tile_mask.T
    send, held, masked = partial_hidden(carried, counts, mask, neighbours, peak_weight)
    held = total([held, between_cores(lax.optimization_barrier(send.astype(LINK)))])
    held, w_in, w_out, gain = lax.optimization_barrier((held, w_in, w_out, gain))
    gain = gain.reshape(1, -1)
    turned = turn(masked)
    steps = chip_steps(n_grp, n_peak)
    for step in steps:
        held = total([held] + [exchange(held, bits) for bits in step])
        if step is steps[-1]:
            held, turned = lax.optimization_barrier((held, turned))
    other = between_cores(held).astype(F32)
    held = held.astype(F32)
    lists = () if carried else (lax.all_gather(neighbours, ALL, axis=0, tiled=True).T,)
    peak_grad, gain_grad, in_grad, out_grad = tower(
        carried, length_of, held, other, turned, gain, w_in, w_out, *lists
    )
    return (peak_grad, gain_grad.reshape(-1), in_grad, out_grad)


def solution(mesh):
    placed = (
        P(None, ALL),
        P(None, ALL),
        P(ALL, None),
        P(ALL, None),
        P(),
        P(),
        P(),
    )
    return jax.shard_map(
        functools.partial(body, mesh.shape["grp"], mesh.shape["peak"]),
        mesh=mesh,
        in_specs=placed,
        out_specs=(P(ALL, None), P(), P(), P()),
        check_vma=False,
    )
```
